512 devices in a mesh: rep: 8 (over z_lo, core), row: 8 (over x, z_hi), col: 8 (over y).
Axes of the slice: x: 4, y: 8, z: 8 (z_hi: 2, z_lo: 4; z = z_hi * 4 + z_lo), core: 2. Of those that a mesh axis runs over, the one named last changes fastest.
Arguments:
- p_vals: bfloat16 [256, 8, 6, 4096], P(('row', 'col'), 'rep'), may hold values from -0.75 to 0.75
- p_cols: int32 [256, 8, 6], P(('row', 'col'), 'rep'), may hold values from 0 to 31, as said below
- f_cols: int32 [256, 8, 8, 2], P(('row', 'col')), may hold values from 0 to 3, as said below
Outputs:
- combined: float32 [256, 8, 8, 2, 4096], P(('row', 'col'), 'rep')
The draws below stay inside these ranges and needn't reach their ends.
Inputs may be any that keep to these rules, and one draw needn't show every extreme that they name: `p_cols`: within one block row and column tile the 6 entries are distinct. `f_cols`: within one block row, column tile and column group the 2 entries are distinct.
All inputs are finite; a program needn't handle non-finite values.
Results may differ from the reference program's by a relative error of at most 0.007.
Values may be sent and summed in bfloat16 or wider, within the bound.
A program may use at most 128 MiB of HBM per device.

```python
import jax
import jax.numpy as jnp
from jax import lax

BS = 64
SLOT = 6
FS = 2
RB = 4
NB = 256
TILE = 32
WIN = 4
N_REP = 8
N_ROW = 8
N_COL = 8


def draw_p_cols(key, part):
    key = jax.random.fold_in(key, 11)
    sub_keys = jax.random.split(key, NB * N_REP)

    def pick_slots(sub_key):
        return jax.random.permutation(sub_key, TILE)[:SLOT]
    chosen_rows = jax.vmap(pick_slots)(sub_keys)
    return chosen_rows.reshape(NB, N_REP, SLOT).astype(jnp.int32)


def draw_f_cols(key, part):
    key = jax.random.fold_in(key, 23)
    sub_keys = jax.random.split(key, NB * N_REP * N_COL)

    def pick_kept(sub_key):
        return jax.random.permutation(sub_key, WIN)[:FS]
    chosen_rows = jax.vmap(pick_kept)(sub_keys)
    return chosen_rows.reshape(NB, N_REP, N_COL, FS).astype(jnp.int32)


def block_levels(key, extent, shards, least, high):
    def one(position, shards_of):
        heights = jax.random.uniform(jax.random.fold_in(jax.random.fold_in(key, 6), position), (shards_of,), jnp.float32, least / len(shards), high / len(shards))
        return jnp.repeat(jnp.exp(heights), extent[position] // shards_of).reshape((-1,) + (1,) * (len(extent) - position - 1))

    loudness = one(*shards[0])
    for cut in shards[1:]:
        loudness = loudness * one(*cut)
    return loudness


def gaussian(key, extent, width, reach, cuts=(), held_as=jnp.bfloat16):
    factor_of = block_levels(key, extent, cuts, -0.22, 0.18) if cuts else 1.0
    drawn = jax.random.normal(key, extent, jnp.float32) * width * factor_of
    return jnp.minimum(jnp.maximum(drawn, -reach), reach).astype(held_as)


def setup_inputs(seed: int = 0) -> dict:
    key_list = jax.random.split(jax.random.key(seed), 4)
    return {
        "p_vals": gaussian(key_list[0], (NB, N_REP, SLOT, BS * BS), BS ** -0.5, 0.75, ((0, 64), (1, 8))),
        "p_cols": draw_p_cols(jax.random.fold_in(key_list[3], 71), 0),
        "f_cols": draw_f_cols(jax.random.fold_in(key_list[3], 71), 0),
    }


def reference(p_vals, p_cols, f_cols):
    groups_tile = N_ROW * N_COL // N_REP
    tile_ids = jnp.arange(N_REP, dtype=jnp.int32)[:, None, None]
    group_ids = jnp.arange(N_COL, dtype=jnp.int32)[None, :, None]
    outputs = N_REP * N_COL * FS

    def one_row(index):
        row_vals = p_vals[index].astype(jnp.float32)
        row_keys = p_cols[index]
        kept = f_cols[index]
        sweep = kept // RB
        target = ((tile_ids * groups_tile + group_ids + sweep * N_COL) * RB + kept % RB).reshape(-1)
        picked = p_vals[target].astype(jnp.float32)
        picked_keys = p_cols[target]
        equal_keys = (row_keys[None, :, :, None] == picked_keys[:, :, None, :]).astype(jnp.float32)
        aligned = jnp.einsum("oqst,oqtv->oqsv", equal_keys, picked)
        left_blocks = row_vals.reshape(N_REP, SLOT, BS, BS)
        right_blocks = aligned.reshape(outputs, N_REP, SLOT, BS, BS)
        layers = jnp.einsum("qsxy,oqszy->oqxz", left_blocks, right_blocks)
        layers = lax.optimization_barrier(layers.astype(jnp.bfloat16)).astype(jnp.float32)
        product = jnp.sum(layers, axis=1).reshape(outputs, BS * BS)
        tile_column = ((group_ids + sweep * N_COL) * RB + kept % RB).reshape(N_REP, N_COL * FS)
        present = (tile_column[:, :, None] == row_keys[:, None, :]).astype(jnp.float32)
        own_entries = jnp.einsum("qos,qsv->qov", present, row_vals).reshape(outputs, BS * BS)
        result = 2.0 * own_entries - product
        return result.reshape(N_REP, N_COL, FS, BS * BS)

    return lax.map(one_row, jnp.arange(NB, dtype=jnp.int32))
```

```python
import functools

import jax
import jax.numpy as jnp
from jax import lax
from jax.experimental import pallas as pl
from jax.experimental.pallas import tpu as pltpu
from jax.sharding import PartitionSpec as P

MESH = pl.DeviceIdType.MESH
BS = 64
TW = 2 * BS
NT = 12
SEC = 25
NX = 4
NZ = 4
NY = 8
RB = 4
SLOT = 6


def kernel(left_ref, right_ref, meta_ref, out_ref,
           lbuf, rtab, otab, lmv, rmv, lms, rms, wbuf, acc, sbuf, rbuf, ysend, yrecv,
           ssem, lr, lmr, rr, rmr, zs, zr, ys, yr, msem):
    rep = lax.axis_index("rep")
    row = lax.axis_index("row")
    y = lax.axis_index("col")
    core = rep % 2
    zl = rep // 2
    zh = row % 2
    x = row // 2
    sib = rep + 1 - 2 * core
    far_row = row + 1 - 2 * zh
    same = core == zh

    def dev(a, b, c):
        return {"rep": a, "row": b, "col": c}

    yp = (y + 1) % NY
    ym = (y + NY - 1) % NY
    xp = (x + 1) % NX
    xm = (x + NX - 1) % NX
    up, down = dev(rep, row, yp), dev(rep, row, ym)
    sibling = dev(sib, row, y)
    xright, xleft = dev(rep, xp * 2 + zh, y), dev(rep, xm * 2 + zh, y)

    partners = [sibling, dev(rep, far_row, y), dev(sib, far_row, y), xright, xleft]
    partners += [dev(rep, row, (y + s) % NY) for s in range(1, NY)]
    partners += [dev((zl + 1) % NZ * 2 + core, row, y), dev((zl + NZ - 1) % NZ * 2 + core, row, y)]
    barrier = pltpu.get_barrier_semaphore()
    for p in partners:
        pl.semaphore_signal(barrier, inc=1, device_id=p, device_id_type=MESH)
    pl.semaphore_wait(barrier, len(partners))

    counter = [0]
    sent = []

    def describe(i, src, dst, rsem, to):
        return pltpu.make_async_remote_copy(
            src_ref=src, dst_ref=dst, send_sem=ssem.at[i], recv_sem=rsem,
            device_id=to, device_id_type=MESH)

    def send(src, dst, rsem, to):
        i = counter[0]
        counter[0] += 1
        describe(i, src, dst, rsem, to).start()
        sent.append((i, src, dst, rsem, to))

    def arrive(dst, rsem):
        pltpu.make_async_remote_copy(
            src_ref=dst, dst_ref=dst, send_sem=ssem.at[0], recv_sem=rsem,
            device_id=sibling, device_id_type=MESH).wait_recv()

    def lslot(yy, t):
        return yy * 2 + t

    def ltiles(s, half=None):
        if half is None:
            return lbuf.at[pl.ds(s * NT, NT)]
        return lbuf.at[pl.ds(s * NT + half * (NT // 2), NT // 2)]

    def rtiles(s):
        return rtab.at[pl.ds(s * SEC, NT)]

    own = lslot(y, core)
    own_sec = x * 2 + core
    send(right_ref, rtiles(own_sec), rr.at[own_sec], dev(zl * 2 + zh, far_row, y))
    send(meta_ref, rmv.at[own_sec], rmr.at[own_sec], dev(zl * 2 + zh, far_row, y))
    sib_mark = counter[0]
    counter[0] += 2

    def to_sibling():
        return (describe(sib_mark, right_ref, rtiles(own_sec), rr.at[own_sec], sibling),
                describe(sib_mark + 1, meta_ref, rmv.at[own_sec], rmr.at[own_sec], sibling))

    @pl.when(jnp.logical_not(same))
    def _():
        for c in to_sibling():
            c.start()

    for to in (up, down, sibling):
        send(left_ref, ltiles(own), lr.at[own, 0], to)
        send(meta_ref, lmv.at[own], lmr.at[own], to)

    lbuf[pl.ds(own * NT, NT)] = left_ref[...]
    lmv[own] = meta_ref[...]
    zero_tile = jnp.zeros((BS, TW), jnp.bfloat16)
    for s in range(2 * NX):
        rtab[s * SEC + 2 * NT] = zero_tile
    otab[2 * NT] = zero_tile

    def swap(v):
        return jnp.concatenate([v[:, BS:], v[:, :BS]], axis=1)

    otab[pl.ds(0, NT)] = left_ref[...]

    def own_swap(i, carry):
        otab[NT + i] = swap(left_ref[i])
        return carry

    lax.fori_loop(0, NT, own_swap, 0)

    base_mark = counter[0]
    counter[0] += 8

    def xcopies():
        i = base_mark
        for t in range(2):
            sec = x * 2 + t
            for to in ((xright, xleft) if t == 0 else (xleft, xright)):
                yield describe(i, rtiles(sec), rtiles(sec), rr.at[sec], to)
                yield describe(i + 1, rmv.at[sec], rmv.at[sec], rmr.at[sec], to)
                i += 2

    def base(first):
        other_sec = x * 2 + 1 - core
        if first:
            rtab[pl.ds(own_sec * SEC, NT)] = right_ref[...]
            rmv[own_sec] = meta_ref[...]
        else:
            arrive(rtiles(own_sec), rr.at[own_sec])
            arrive(rmv.at[own_sec], rmr.at[own_sec])
        arrive(rtiles(other_sec), rr.at[other_sec])
        arrive(rmv.at[other_sec], rmr.at[other_sec])
        for c in xcopies():
            c.start()

    @pl.when(same)
    def _():
        base(True)

    def lstep(s):
        a = lslot((y + NY - s) % NY, core)
        b = lslot((y + s) % NY, core)
        for slot, to, half in ((a, up, 0), (b, down, 1)):
            arrive(ltiles(slot), lr.at[slot, 0])
            if s < 3:
                send(ltiles(slot), ltiles(slot), lr.at[slot, 0], to)
            else:
                send(ltiles(slot, half), ltiles(slot, half), lr.at[slot, half], to)
            send(ltiles(slot), ltiles(slot), lr.at[slot, 0], sibling)
            arrive(lmv.at[slot], lmr.at[slot])
            if s < 3 or half == 0:
                send(lmv.at[slot], lmv.at[slot], lmr.at[slot], to)
            send(lmv.at[slot], lmv.at[slot], lmr.at[slot], sibling)

    lstep(1)
    lstep(2)

    @pl.when(jnp.logical_not(same))
    def _():
        base(False)

    lstep(3)

    def rhop(src_x, t, to):
        sec = src_x * 2 + t
        arrive(rtiles(sec), rr.at[sec])
        arrive(rmv.at[sec], rmr.at[sec])
        if to is not None:
            send(rtiles(sec), rtiles(sec), rr.at[sec], to)
            send(rmv.at[sec], rmv.at[sec], rmr.at[sec], to)

    rhop(xm, 0, xright)
    rhop(xp, 1, xleft)
    rhop(xm, 1, None)
    rhop(xp, 0, None)

    far = lslot((y + 4) % NY, core)
    for half in range(2):
        arrive(ltiles(far, half), lr.at[far, half])
        send(ltiles(far, half), ltiles(far, half), lr.at[far, half], sibling)
    arrive(lmv.at[far], lmr.at[far])
    send(lmv.at[far], lmv.at[far], lmr.at[far], sibling)

    def widen(xx):
        def body(i, carry):
            first = xx * 2 * SEC + i
            rtab[first + NT] = swap(rtab[first])
            rtab[first + SEC + NT] = swap(rtab[first + SEC])
            return carry
        lax.fori_loop(0, NT, body, 0)

    widen(x)
    widen(xm)
    widen(xp)
    x2 = (x + 2) % NX
    rhop(x2, 0, None)
    rhop(x2, 1, None)
    widen(x2)

    rm_copy = pltpu.make_async_copy(rmv, rms, msem.at[0])
    rm_copy.start()
    for s in range(NY):
        slot = lslot((y + s) % NY, 1 - core)
        arrive(lmv.at[slot], lmr.at[slot])
    lm_copy = pltpu.make_async_copy(lmv, lms, msem.at[1])
    lm_copy.start()
    for s in range(NY):
        slot = lslot((y + s) % NY, 1 - core)
        if s == 4:
            for half in range(2):
                arrive(ltiles(slot, half), lr.at[slot, half])
        else:
            arrive(ltiles(slot), lr.at[slot, 0])
    rm_copy.wait()
    lm_copy.wait()

    lane = lax.broadcasted_iota(jnp.int32, (BS, TW), 1)
    low = lane < BS

    def group_of(n):
        away = (n + 1) // 2
        return (y + jnp.where(n % 2 == 1, NY - away, away)) % NY

    def compute(n):
        g = group_of(n)
        for rb in range(RB):
            tiles = []
            for t in range(2):
                for pair in range(3):
                    tiles.append(lbuf[(g * 2 + t) * NT + rb * 3 + pair])
            lhs = jnp.concatenate(tiles, axis=1)
            keys = [lms[g * 2 + t, 6, rb * SLOT + s] for t in range(2) for s in range(SLOT)]
            for d in range(NZ):
                at = (2 * d + core) * 16 + y * 2
                j0 = lms[g * 2, rb, at] * 32
                j1 = lms[g * 2, rb, at + 1] * 32
                for t in range(2):
                    sec = d * 2 + t
                    for s in range(SLOT):
                        k = keys[t * SLOT + s]
                        lo = rtab[sec * SEC + rms[sec, 4, j0 + k]]
                        hi = rtab[sec * SEC + rms[sec, 5, j1 + k]]
                        wbuf[rb % 2, pl.ds((t * SLOT + s) * BS, BS), pl.ds(d * TW, TW)] = jnp.where(low, lo, hi)
            res = jnp.dot(lhs, wbuf[rb % 2], preferred_element_type=jnp.float32)
            for d in range(NZ):
                acc[n * NZ + d, pl.ds(rb * BS, BS), :] = res[:, d * TW:(d + 1) * TW]

    def zcopy(n, d):
        right = d > zl
        side = jnp.where(right, 0, 1)
        nxt = jnp.where(right, zl + 1, zl - 1)
        return pltpu.make_async_remote_copy(
            src_ref=sbuf.at[n * NZ + d], dst_ref=rbuf.at[side, n * NZ + d],
            send_sem=zs.at[n * NZ + d], recv_sem=zr.at[side, n * NZ + d],
            device_id=dev(nxt * 2 + core, row, y), device_id_type=MESH)

    def reduce_on(n):
        for step in range(NZ):
            d = jnp.where(zl < 2, NZ - 1 - step, step)
            right = d > zl
            side = jnp.where(right, 0, 1)
            hears = jnp.logical_or(jnp.logical_and(right, zl > 0), jnp.logical_and(d < zl, zl < NZ - 1))

            @pl.when(d != zl)
            def _():
                @pl.when(hears)
                def _():
                    arrive(rbuf.at[side, n * NZ + d], zr.at[side, n * NZ + d])
                    sbuf[n * NZ + d] = (acc[n * NZ + d] + rbuf[side, n * NZ + d].astype(jnp.float32)).astype(jnp.bfloat16)

                @pl.when(jnp.logical_not(hears))
                def _():
                    sbuf[n * NZ + d] = acc[n * NZ + d].astype(jnp.bfloat16)

                zcopy(n, d).start()

    def ycopy(n):
        return pltpu.make_async_remote_copy(
            src_ref=ysend.at[n], dst_ref=yrecv.at[y], send_sem=ys.at[n], recv_sem=yr.at[y],
            device_id=dev(rep, row, group_of(n)), device_id_type=MESH)

    def finish(n):
        at = n * NZ + zl

        @pl.when(zl > 0)
        def _():
            arrive(rbuf.at[0, at], zr.at[0, at])
            acc[at] = acc[at] + rbuf[0, at].astype(jnp.float32)

        @pl.when(zl < NZ - 1)
        def _():
            arrive(rbuf.at[1, at], zr.at[1, at])
            acc[at] = acc[at] + rbuf[1, at].astype(jnp.float32)

        total = acc[at].astype(jnp.bfloat16)

        @pl.when(n == 0)
        def _():
            yrecv[y] = total

        @pl.when(n > 0)
        def _():
            ysend[n] = total
            ycopy(n).start()

    def main(n, carry):
        @pl.when(n < NY)
        def _():
            compute(n)
            reduce_on(n)

        @pl.when(n >= 2)
        def _():
            finish(n - 2)
        return carry

    lax.fori_loop(0, NY + 2, main, 0)

    par = lax.broadcasted_iota(jnp.int32, (BS, TW), 0) % 2
    half_of = lane // BS

    def combine(s, carry):
        c = group_of(s)

        @pl.when(s > 0)
        def _():
            arrive(yrecv.at[c], yr.at[c])

        for rb in range(RB):
            at = rep * 16 + c * 2
            k0 = rb * 32 + c * RB + lms[own, rb, at]
            k1 = rb * 32 + c * RB + lms[own, rb, at + 1]
            mine = jnp.where(low, otab[lms[own, 4, k0]].astype(jnp.float32), otab[lms[own, 5, k1]].astype(jnp.float32))
            m = 2.0 * mine - yrecv[c, pl.ds(rb * BS, BS), :].astype(jnp.float32)
            turned = pltpu.roll(m, BS, 1)
            out_ref[rb * NY + c] = jnp.where(
                par == half_of, m,
                jnp.where(par == 0, pltpu.roll(turned, BS - 1, 0), pltpu.roll(turned, 1, 0)))
        return carry

    lax.fori_loop(0, NY, combine, 0)

    for c in sent:
        describe(*c).wait_send()
    for c in xcopies():
        c.wait_send()

    @pl.when(jnp.logical_not(same))
    def _():
        for c in to_sibling():
            c.wait_send()

    def drain(n, carry):
        for d in range(NZ):
            @pl.when(zl != d)
            def _():
                zcopy(n, d).wait_send()

        @pl.when(n > 0)
        def _():
            ycopy(n).wait_send()
        return carry

    lax.fori_loop(0, NY, drain, 0)


def local(p_vals, p_cols, f_cols):
    vals = p_vals.reshape(RB, 3, 2, BS, BS)
    left = vals.transpose(0, 1, 3, 2, 4).reshape(NT, BS, TW)
    right = vals.transpose(0, 1, 4, 2, 3).reshape(NT, BS, TW)
    keys = p_cols[:, 0]
    slot = jnp.arange(SLOT, dtype=jnp.int32)[None]
    place = jnp.arange(RB, dtype=jnp.int32)[:, None] * 3 + slot // 2
    hit = keys[:, None, :] == jnp.arange(32, dtype=jnp.int32)[None, :, None]
    lo = jnp.min(jnp.where(hit, (place + slot % 2 * NT)[:, None], 2 * NT), axis=2)
    hi = jnp.min(jnp.where(hit, (place + (1 - slot % 2) * NT)[:, None], 2 * NT), axis=2)
    meta = jnp.concatenate([
        f_cols.reshape(RB, 128), lo.reshape(1, 128), hi.reshape(1, 128),
        jnp.pad(keys.reshape(1, RB * SLOT), ((0, 1), (0, 128 - RB * SLOT)))], axis=0)

    vm = pl.BlockSpec(memory_space=pltpu.VMEM)
    bf, f32 = jnp.bfloat16, jnp.float32
    out = pl.pallas_call(
        kernel,
        out_shape=jax.ShapeDtypeStruct((RB * NY, BS, TW), f32),
        in_specs=[vm] * 3,
        out_specs=vm,
        scratch_shapes=[
            pltpu.VMEM((2 * NY * NT, BS, TW), bf),
            pltpu.VMEM((2 * NX * SEC, BS, TW), bf),
            pltpu.VMEM((SEC, BS, TW), bf),
            pltpu.VMEM((2 * NY, 8, 128), jnp.int32),
            pltpu.VMEM((2 * NX, 8, 128), jnp.int32),
            pltpu.SMEM((2 * NY, 8, 128), jnp.int32),
            pltpu.SMEM((2 * NX, 8, 128), jnp.int32),
            pltpu.VMEM((2, 2 * SLOT * BS, NZ * TW), bf),
            pltpu.VMEM((NY * NZ, RB * BS, TW), f32),
            pltpu.VMEM((NY * NZ, RB * BS, TW), bf),
            pltpu.VMEM((2, NY * NZ, RB * BS, TW), bf),
            pltpu.VMEM((NY, RB * BS, TW), bf),
            pltpu.VMEM((NY, RB * BS, TW), bf),
            pltpu.SemaphoreType.DMA((64,)),
            pltpu.SemaphoreType.DMA((2 * NY, 2)),
            pltpu.SemaphoreType.DMA((2 * NY,)),
            pltpu.SemaphoreType.DMA((2 * NX,)),
            pltpu.SemaphoreType.DMA((2 * NX,)),
            pltpu.SemaphoreType.DMA((NY * NZ,)),
            pltpu.SemaphoreType.DMA((2, NY * NZ)),
            pltpu.SemaphoreType.DMA((NY,)),
            pltpu.SemaphoreType.DMA((NY,)),
            pltpu.SemaphoreType.DMA((2,)),
        ],
        compiler_params=pltpu.CompilerParams(
            collective_id=0, has_side_effects=True, vmem_limit_bytes=48 * 1024 * 1024),
    )(left, right, meta)
    out = out.reshape(RB, NY, BS // 2, 2, TW).transpose(0, 1, 3, 2, 4)
    return out.reshape(RB, 1, NY, 2, BS * BS)


def solution(mesh):
    return jax.shard_map(
        local,
        mesh=mesh,
        in_specs=(
            P(("row", "col"), "rep", None, None),
            P(("row", "col"), "rep", None),
            P(("row", "col"), None, None, None),
        ),
        out_specs=P(("row", "col"), "rep", None, None, None),
        check_vma=False,
    )
```

```python
import functools

import jax
import jax.numpy as jnp
from jax import lax
from jax.experimental import pallas as pl
from jax.experimental.pallas import tpu as pltpu
from jax.sharding import PartitionSpec as P

MESH = pl.DeviceIdType.MESH
BS = 64
TW = 2 * BS
NT = 12
SEC = 25
NX = 4
NZ = 4
NY = 8
RB = 4
SLOT = 6
LAG = 2


def kernel(left_ref, right_ref, meta_ref, out_ref,
           lbuf, rtab, otab, lmv, rmv, lms, rms, oms, wbuf, keep, sbuf, rbuf, ysend, yrecv,
           ssem, lr, lmr, rr, rmr, zs, zr, ys, yr, msem):
    rep = lax.axis_index("rep")
    row = lax.axis_index("row")
    y = lax.axis_index("col")
    core = rep % 2
    zl = rep // 2
    zh = row % 2
    x = row // 2
    zp = zl % 2
    other = 1 - core
    zn = zl + 1 - 2 * zp
    zf = (zl + 2) % NZ
    far_row = row + 1 - 2 * zh
    is_base = x % 2 == zp
    same = core == zh
    keeps_own = jnp.logical_and(is_base, same)

    def dev(a, b, c):
        return {"rep": a, "row": b, "col": c}

    xp = (x + 1) % NX
    xm = (x + NX - 1) % NX
    up, down = dev(rep, row, (y + 1) % NY), dev(rep, row, (y + NY - 1) % NY)
    sibling = dev(zl * 2 + other, row, y)
    z_next = dev(zn * 2 + core, row, y)
    z_far = dev(zf * 2 + core, row, y)
    xright, xleft = dev(rep, xp * 2 + zh, y), dev(rep, xm * 2 + zh, y)

    partners = [xright, xleft, z_far]
    for r in (row, far_row):
        for z in (zl, zn):
            for c in (core, other):
                if not (r is row and z is zl and c is core):
                    partners.append(dev(z * 2 + c, r, y))
    partners += [dev(rep, row, (y + s) % NY) for s in range(1, NY)]
    barrier = pltpu.get_barrier_semaphore()
    for p in partners:
        pl.semaphore_signal(barrier, inc=1, device_id=p, device_id_type=MESH)
    pl.semaphore_wait(barrier, len(partners))

    counter = [0]
    sent = []

    def describe(i, src, dst, rsem, to):
        return pltpu.make_async_remote_copy(
            src_ref=src, dst_ref=dst, send_sem=ssem.at[i], recv_sem=rsem,
            device_id=to, device_id_type=MESH)

    def take(count):
        first = counter[0]
        counter[0] += count
        return first

    def send(src, dst, rsem, to):
        i = take(1)
        describe(i, src, dst, rsem, to).start()
        sent.append((i, src, dst, rsem, to))

    def arrive(dst, rsem):
        pltpu.make_async_remote_copy(
            src_ref=dst, dst_ref=dst, send_sem=ssem.at[0], recv_sem=rsem,
            device_id=sibling, device_id_type=MESH).wait_recv()

    def lslot(yy, c, q):
        return (yy * 2 + c) * 2 + q

    def ltiles(s):
        return lbuf.at[pl.ds(s * NT, NT)]

    def rtiles(s):
        return rtab.at[pl.ds(s * SEC, NT)]

    def rsec(xx, c, q):
        return xx // 2 * 4 + c * 2 + q

    own = lslot(y, core, zp)
    own_sec = rsec(x, core, zp)
    zt = jnp.where(is_base, zl, zn)
    base_far = dev(zt * 2 + zh, far_row, y)
    base_near = dev(zt * 2 + zh, row, y)
    near_mark = take(2)

    def near_copies():
        return (describe(near_mark, right_ref, rtiles(own_sec), rr.at[own_sec], base_near),
                describe(near_mark + 1, meta_ref, rmv.at[own_sec], rmr.at[own_sec], base_near))

    send(right_ref, rtiles(own_sec), rr.at[own_sec], base_far)
    send(meta_ref, rmv.at[own_sec], rmr.at[own_sec], base_far)

    @pl.when(jnp.logical_not(keeps_own))
    def _():
        for c in near_copies():
            c.start()

    def lsend(src, msrc, slot, to):
        send(src, ltiles(slot), lr.at[slot], to)
        send(msrc, lmv.at[slot], lmr.at[slot], to)

    for to in (z_next, up, down, sibling):
        lsend(left_ref, meta_ref, own, to)

    order = [(core, zp), (other, zp), (core, 1 - zp), (other, 1 - zp)]
    base_mark = take(16)

    def xcopies(k):
        sec = rsec(x, *order[k])
        i = base_mark + 4 * k
        for to in ((xright, xleft) if k % 2 == 0 else (xleft, xright)):
            yield describe(i, rtiles(sec), rtiles(sec), rr.at[sec], to)
            yield describe(i + 1, rmv.at[sec], rmv.at[sec], rmr.at[sec], to)
            i += 2

    def rarrive(sec):
        arrive(rtiles(sec), rr.at[sec])
        arrive(rmv.at[sec], rmr.at[sec])

    def base(ks):
        for k in ks:
            rarrive(rsec(x, *order[k]))
            for c in xcopies(k):
                c.start()

    @pl.when(keeps_own)
    def _():
        rtab[pl.ds(own_sec * SEC, NT)] = right_ref[...]
        rmv[own_sec] = meta_ref[...]
        for c in xcopies(0):
            c.start()

    lbuf[pl.ds(own * NT, NT)] = left_ref[...]
    lmv[own] = meta_ref[...]
    zero_tile = jnp.zeros((BS, TW), jnp.bfloat16)
    for s in range(8):
        rtab[s * SEC + 2 * NT] = zero_tile
    otab[2 * NT] = zero_tile

    def swap(v):
        return jnp.concatenate([v[:, BS:], v[:, :BS]], axis=1)

    for i in range(NT):
        v = left_ref[i]
        otab[i] = v
        otab[NT + i] = swap(v)

    def larrive(slot):
        arrive(ltiles(slot), lr.at[slot])
        arrive(lmv.at[slot], lmr.at[slot])

    def lpass(slot, to):
        lsend(ltiles(slot), lmv.at[slot], slot, to)

    marks = {1: take(16), 2: take(16), 3: take(12), 4: take(4)}

    def lring(s):
        i = marks[s]
        for q, half in ((zp, 0), (1 - zp, 1)):
            for yy, to, way in (((y + NY - s) % NY, up, 0), ((y + s) % NY, down, 1)):
                if s == 4 and way == 1:
                    continue
                slot = lslot(yy, core, q)
                goals = [to] if s < 3 or (s == 3 and half == way) else []
                copies = []
                for goal in goals + [sibling]:
                    copies.append(describe(i, ltiles(slot), ltiles(slot), lr.at[slot], goal))
                    copies.append(describe(i + 1, lmv.at[slot], lmv.at[slot], lmr.at[slot], goal))
                    i += 2
                yield slot, copies

    def lstep(s):
        for slot, copies in lring(s):
            larrive(slot)
            for c in copies:
                c.start()

    hop_mark = take(8)

    def hops(k):
        sec = rsec(xm if k % 2 == 0 else xp, *order[k])
        to = xright if k % 2 == 0 else xleft
        return (sec, describe(hop_mark + 2 * k, rtiles(sec), rtiles(sec), rr.at[sec], to),
                describe(hop_mark + 2 * k + 1, rmv.at[sec], rmv.at[sec], rmr.at[sec], to))

    def hop_on(ks):
        for k in ks:
            sec, a, b = hops(k)
            rarrive(sec)
            a.start()
            b.start()

    no_base = jnp.logical_not(is_base)
    differs = jnp.logical_not(same)

    @pl.when(keeps_own)
    def _():
        base((1, 2, 3))

    pair = lslot(y, core, 1 - zp)
    larrive(pair)
    for to in (up, down, sibling):
        lpass(pair, to)

    @pl.when(jnp.logical_and(is_base, differs))
    def _():
        base((0, 1, 2, 3))

    @pl.when(jnp.logical_and(no_base, same))
    def _():
        hop_on((0, 1, 2, 3))

    lstep(1)

    @pl.when(jnp.logical_and(no_base, differs))
    def _():
        hop_on((0, 1))

    @pl.when(differs)
    def _():
        lstep(2)

    @pl.when(jnp.logical_and(no_base, differs))
    def _():
        hop_on((2, 3))

    @pl.when(no_base)
    def _():
        for k in range(4):
            rarrive(rsec(xp if k % 2 == 0 else xm, *order[k]))

    @pl.when(is_base)
    def _():
        for k in range(4):
            rarrive(rsec((x + 2) % NX, *order[k]))

    rm_copy = pltpu.make_async_copy(rmv, rms, msem.at[0])
    rm_copy.start()
    om_copy = pltpu.make_async_copy(meta_ref, oms, msem.at[2])
    om_copy.start()

    def widen(sec, carry):
        for i in range(NT):
            rtab[sec * SEC + NT + i] = swap(rtab[sec * SEC + i])
        return carry

    lax.fori_loop(0, 8, widen, 0)

    lane = lax.broadcasted_iota(jnp.int32, (BS, TW), 1)
    low = lane < BS

    def group_of(n):
        away = (n + 1) // 2
        return (y + jnp.where(n % 2 == 1, NY - away, away)) % NY

    def meta_copy(n):
        g = group_of(n)
        return pltpu.make_async_copy(lmv.at[pl.ds(g * 4, 4)], lms.at[pl.ds(g * 4, 4)], msem.at[1])

    def meta_in(n):
        g = group_of(n)
        for q in range(2):
            slot = lslot(g, other, q)
            arrive(lmv.at[slot], lmr.at[slot])
        meta_copy(n).start()

    def compute(n):
        g = group_of(n)
        for q in range(2):
            slot = lslot(g, other, q)
            arrive(ltiles(slot), lr.at[slot])
        dests = (zl, zf)
        for rb in range(RB):
            tiles = [lbuf[(g * 4 + t) * NT + rb * 3 + p] for t in range(4) for p in range(3)]
            lhs = jnp.concatenate(tiles, axis=1)
            keys = [lms[g * 4 + t, 4 + rb, 64 + s] for t in range(4) for s in range(SLOT)]
            for i, d in enumerate(dests):
                at = (2 * d + core) * 16 + y * 2
                j0 = lms[g * 4, rb, at] + 4
                j1 = lms[g * 4, rb, at + 1] + 4
                for t in range(4):
                    sec = d // 2 * 4 + t
                    for s in range(SLOT):
                        k = keys[t * SLOT + s]
                        lo = rtab[sec * SEC + rms[sec, j0, k]]
                        hi = rtab[sec * SEC + rms[sec, j1, k + 32]]
                        wbuf[rb % 2, pl.ds((t * SLOT + s) * BS, BS), pl.ds(i * TW, TW)] = jnp.where(low, lo, hi)
            res = jnp.dot(lhs, wbuf[rb % 2], preferred_element_type=jnp.float32)
            keep[n, pl.ds(rb * BS, BS), :] = res[:, :TW]
            sbuf[n, pl.ds(rb * BS, BS), :] = res[:, TW:].astype(jnp.bfloat16)

    def zcopy(n):
        return pltpu.make_async_remote_copy(
            src_ref=sbuf.at[n], dst_ref=rbuf.at[n], send_sem=zs.at[n], recv_sem=zr.at[n],
            device_id=z_far, device_id_type=MESH)

    def ycopy(n):
        return pltpu.make_async_remote_copy(
            src_ref=ysend.at[n], dst_ref=yrecv.at[y], send_sem=ys.at[n], recv_sem=yr.at[y],
            device_id=dev(rep, row, group_of(n)), device_id_type=MESH)

    def finish(n):
        arrive(rbuf.at[n], zr.at[n])
        total = (keep[n] + rbuf[n].astype(jnp.float32)).astype(jnp.bfloat16)

        @pl.when(n == 0)
        def _():
            yrecv[y] = total

        @pl.when(n > 0)
        def _():
            ysend[n] = total
            ycopy(n).start()

    par = lax.broadcasted_iota(jnp.int32, (BS, TW), 0) % 2
    half_of = lane // BS

    def combine(s):
        c = group_of(s)

        @pl.when(s > 0)
        def _():
            arrive(yrecv.at[c], yr.at[c])

        for rb in range(RB):
            at = rep * 16 + c * 2
            k0 = c * RB + oms[rb, at]
            k1 = 32 + c * RB + oms[rb, at + 1]
            mine = jnp.where(low, otab[oms[4 + rb, k0]].astype(jnp.float32),
                             otab[oms[4 + rb, k1]].astype(jnp.float32))
            m = 2.0 * mine - yrecv[c, pl.ds(rb * BS, BS), :].astype(jnp.float32)
            turned = pltpu.roll(m, BS, 1)
            out_ref[rb * NY + c] = jnp.where(
                par == half_of, m,
                jnp.where(par == 0, pltpu.roll(turned, BS - 1, 0), pltpu.roll(turned, 1, 0)))

    meta_in(0)
    rm_copy.wait()
    om_copy.wait()

    def main(n, carry):
        @pl.when(n < NY)
        def _():
            meta_copy(n).wait()

            @pl.when(jnp.logical_and(n == 1, same))
            def _():
                lstep(2)

            @pl.when(n == 3)
            def _():
                lstep(3)

            @pl.when(n == 5)
            def _():
                lstep(4)

            @pl.when(n < NY - 1)
            def _():
                meta_in(n + 1)

            compute(n)
            zcopy(n).start()

        @pl.when(jnp.logical_and(n >= LAG, n < NY + LAG))
        def _():
            finish(n - LAG)

        @pl.when(n >= 2 * LAG)
        def _():
            combine(n - 2 * LAG)
        return carry

    lax.fori_loop(0, NY + 2 * LAG, main, 0)

    for c in sent:
        describe(*c).wait_send()
    for s in range(1, 5):
        for slot, copies in lring(s):
            for c in copies:
                c.wait_send()

    @pl.when(jnp.logical_not(keeps_own))
    def _():
        for c in near_copies():
            c.wait_send()

    @pl.when(is_base)
    def _():
        for k in range(4):
            for c in xcopies(k):
                c.wait_send()

    @pl.when(jnp.logical_not(is_base))
    def _():
        for k in range(4):
            sec, a, b = hops(k)
            a.wait_send()
            b.wait_send()

    def drain(n, carry):
        zcopy(n).wait_send()

        @pl.when(n > 0)
        def _():
            ycopy(n).wait_send()
        return carry

    lax.fori_loop(0, NY, drain, 0)


def local(p_vals, p_cols, f_cols):
    vals = p_vals.reshape(RB, 3, 2, BS, BS)
    left = vals.transpose(0, 1, 3, 2, 4).reshape(NT, BS, TW)
    right = vals.transpose(0, 1, 4, 2, 3).reshape(NT, BS, TW)
    keys = p_cols[:, 0]
    slot = jnp.arange(SLOT, dtype=jnp.int32)[None]
    place = jnp.arange(RB, dtype=jnp.int32)[:, None] * 3 + slot // 2
    hit = keys[:, None, :] == jnp.arange(32, dtype=jnp.int32)[None, :, None]
    lo = jnp.min(jnp.where(hit, (place + slot % 2 * NT)[:, None], 2 * NT), axis=2)
    hi = jnp.min(jnp.where(hit, (place + (1 - slot % 2) * NT)[:, None], 2 * NT), axis=2)
    row_data = jnp.concatenate([lo, hi, jnp.pad(keys, ((0, 0), (0, 64 - SLOT)))], axis=1)
    meta = jnp.concatenate([f_cols.reshape(RB, 128), row_data], axis=0)

    vm = pl.BlockSpec(memory_space=pltpu.VMEM)
    bf, f32 = jnp.bfloat16, jnp.float32
    out = pl.pallas_call(
        kernel,
        out_shape=jax.ShapeDtypeStruct((RB * NY, BS, TW), f32),
        in_specs=[vm] * 3,
        out_specs=vm,
        scratch_shapes=[
            pltpu.VMEM((4 * NY * NT, BS, TW), bf),
            pltpu.VMEM((8 * SEC, BS, TW), bf),
            pltpu.VMEM((SEC, BS, TW), bf),
            pltpu.VMEM((4 * NY, 8, 128), jnp.int32),
            pltpu.VMEM((8, 8, 128), jnp.int32),
            pltpu.SMEM((4 * NY, 8, 128), jnp.int32),
            pltpu.SMEM((8, 8, 128), jnp.int32),
            pltpu.SMEM((8, 128), jnp.int32),
            pltpu.VMEM((2, 4 * SLOT * BS, 2 * TW), bf),
            pltpu.VMEM((NY, RB * BS, TW), f32),
            pltpu.VMEM((NY, RB * BS, TW), bf),
            pltpu.VMEM((NY, RB * BS, TW), bf),
            pltpu.VMEM((NY, RB * BS, TW), bf),
            pltpu.VMEM((NY, RB * BS, TW), bf),
            pltpu.SemaphoreType.DMA((112,)),
            pltpu.SemaphoreType.DMA((4 * NY,)),
            pltpu.SemaphoreType.DMA((4 * NY,)),
            pltpu.SemaphoreType.DMA((8,)),
            pltpu.SemaphoreType.DMA((8,)),
            pltpu.SemaphoreType.DMA((NY,)),
            pltpu.SemaphoreType.DMA((NY,)),
            pltpu.SemaphoreType.DMA((NY,)),
            pltpu.SemaphoreType.DMA((NY,)),
            pltpu.SemaphoreType.DMA((3,)),
        ],
        compiler_params=pltpu.CompilerParams(
            collective_id=0, has_side_effects=True, vmem_limit_bytes=48 * 1024 * 1024),
    )(left, right, meta)
    out = out.reshape(RB, NY, BS // 2, 2, TW).transpose(0, 1, 3, 2, 4)
    return out.reshape(RB, 1, NY, 2, BS * BS)


def solution(mesh):
    return jax.shard_map(
        local,
        mesh=mesh,
        in_specs=(
            P(("row", "col"), "rep", None, None),
            P(("row", "col"), "rep", None),
            P(("row", "col"), None, None, None),
        ),
        out_specs=P(("row", "col"), "rep", None, None, None),
        check_vma=False,
    )
```

```python
import functools

import jax
import jax.numpy as jnp
from jax import lax
from jax.experimental import pallas as pl
from jax.experimental.pallas import tpu as pltpu
from jax.sharding import PartitionSpec as P

MESH = pl.DeviceIdType.MESH
BS = 64
TW = 2 * BS
NT = 12
SEC = 25
NX = 4
NZ = 4
NY = 8
RB = 4
SLOT = 6
LAG = 2


def kernel(left_ref, right_ref, meta_ref, out_ref,
           lbuf, rtab, otab, lmv, rmv, lms, rms, oms, wbuf, keep, sbuf, rbuf, ysend, yrecv,
           ssem, lr, lmr, rr, rmr, zs, zr, ys, yr, msem):
    rep = lax.axis_index("rep")
    row = lax.axis_index("row")
    y = lax.axis_index("col")
    core = rep % 2
    zl = rep // 2
    zh = row % 2
    x = row // 2
    zp = zl % 2
    other = 1 - core
    zn = zl + 1 - 2 * zp
    zf = (zl + 2) % NZ
    far_row = row + 1 - 2 * zh
    is_base = x % 2 == zp
    same = core == zh
    keeps_own = jnp.logical_and(is_base, same)

    def dev(a, b, c):
        return {"rep": a, "row": b, "col": c}

    xp = (x + 1) % NX
    xm = (x + NX - 1) % NX
    up, down = dev(rep, row, (y + 1) % NY), dev(rep, row, (y + NY - 1) % NY)
    sibling = dev(zl * 2 + other, row, y)
    z_next = dev(zn * 2 + core, row, y)
    z_far = dev(zf * 2 + core, row, y)
    xright, xleft = dev(rep, xp * 2 + zh, y), dev(rep, xm * 2 + zh, y)

    partners = [xright, xleft, z_far]
    for r in (row, far_row):
        for z in (zl, zn):
            for c in (core, other):
                if not (r is row and z is zl and c is core):
                    partners.append(dev(z * 2 + c, r, y))
    partners += [dev(rep, row, (y + s) % NY) for s in range(1, NY)]
    barrier = pltpu.get_barrier_semaphore()
    for p in partners:
        pl.semaphore_signal(barrier, inc=1, device_id=p, device_id_type=MESH)
    pl.semaphore_wait(barrier, len(partners))

    counter = [0]
    sent = []

    def describe(i, src, dst, rsem, to):
        return pltpu.make_async_remote_copy(
            src_ref=src, dst_ref=dst, send_sem=ssem.at[i], recv_sem=rsem,
            device_id=to, device_id_type=MESH)

    def take(count):
        first = counter[0]
        counter[0] += count
        return first

    def send(src, dst, rsem, to):
        i = take(1)
        describe(i, src, dst, rsem, to).start()
        sent.append((i, src, dst, rsem, to))

    def arrive(dst, rsem):
        pltpu.make_async_remote_copy(
            src_ref=dst, dst_ref=dst, send_sem=ssem.at[0], recv_sem=rsem,
            device_id=sibling, device_id_type=MESH).wait_recv()

    def lslot(yy, c, q):
        return (yy * 2 + c) * 2 + q

    def ltiles(s, h):
        return lbuf.at[pl.ds(s * NT + h * (NT // 2), NT // 2)]

    def rtiles(s):
        return rtab.at[pl.ds(s * SEC, NT)]

    def rsec(xx, c, q):
        return xx // 2 * 4 + c * 2 + q

    own = lslot(y, core, zp)
    own_sec = rsec(x, core, zp)
    zt = jnp.where(is_base, zl, zn)
    base_far = dev(zt * 2 + zh, far_row, y)
    base_near = dev(zt * 2 + zh, row, y)
    near_mark = take(2)

    def near_copies():
        return (describe(near_mark, right_ref, rtiles(own_sec), rr.at[own_sec], base_near),
                describe(near_mark + 1, meta_ref, rmv.at[own_sec], rmr.at[own_sec], base_near))

    send(right_ref, rtiles(own_sec), rr.at[own_sec], base_far)
    send(meta_ref, rmv.at[own_sec], rmr.at[own_sec], base_far)

    @pl.when(jnp.logical_not(keeps_own))
    def _():
        for c in near_copies():
            c.start()

    def lsend_own(to):
        for h in range(2):
            send(left_ref.at[pl.ds(h * (NT // 2), NT // 2)], ltiles(own, h), lr.at[own, h], to)
            if h == 0:
                send(meta_ref, lmv.at[own], lmr.at[own], to)

    for to in (up, down, sibling):
        lsend_own(to)

    order = [(core, zp), (other, zp), (core, 1 - zp), (other, 1 - zp)]
    base_mark = take(16)

    def xcopies(k):
        sec = rsec(x, *order[k])
        i = base_mark + 4 * k
        for to in ((xright, xleft) if k % 2 == 0 else (xleft, xright)):
            yield describe(i, rtiles(sec), rtiles(sec), rr.at[sec], to)
            yield describe(i + 1, rmv.at[sec], rmv.at[sec], rmr.at[sec], to)
            i += 2

    def rarrive(sec):
        arrive(rtiles(sec), rr.at[sec])
        arrive(rmv.at[sec], rmr.at[sec])

    def base(ks):
        for k in ks:
            rarrive(rsec(x, *order[k]))
            for c in xcopies(k):
                c.start()

    @pl.when(keeps_own)
    def _():
        rtab[pl.ds(own_sec * SEC, NT)] = right_ref[...]
        rmv[own_sec] = meta_ref[...]
        for c in xcopies(0):
            c.start()

    lbuf[pl.ds(own * NT, NT)] = left_ref[...]
    lmv[own] = meta_ref[...]
    zero_tile = jnp.zeros((BS, TW), jnp.bfloat16)
    for s in range(8):
        rtab[s * SEC + 2 * NT] = zero_tile
    otab[2 * NT] = zero_tile

    def swap(v):
        return jnp.concatenate([v[:, BS:], v[:, :BS]], axis=1)

    for i in range(NT):
        v = left_ref[i]
        otab[i] = v
        otab[NT + i] = swap(v)

    def larrive(slot, h):
        arrive(ltiles(slot, h), lr.at[slot, h])
        if h == 0:
            arrive(lmv.at[slot], lmr.at[slot])

    marks = {1: take(32), 2: take(32), 3: take(24), 4: take(8)}

    def lring(s, part=None):
        i = marks[s]
        for q, tile in ((zp, 0), (1 - zp, 1)):
            for h in range(2):
                for yy, to, way in (((y + NY - s) % NY, up, 0), ((y + s) % NY, down, 1)):
                    if s == 4 and way != h:
                        continue
                    slot = lslot(yy, core, q)
                    goals = [to] if s < 3 or (s == 3 and h == way) else []
                    copies = []
                    for goal in goals + [sibling]:
                        if part is None or tile == part:
                            copies.append(describe(i, ltiles(slot, h), ltiles(slot, h), lr.at[slot, h], goal))
                            if h == 0:
                                copies.append(describe(i + 1, lmv.at[slot], lmv.at[slot], lmr.at[slot], goal))
                        i += 2
                    if copies:
                        yield h, slot, copies

    def lstep(s, part=None):
        for h, slot, copies in lring(s, part):
            larrive(slot, h)
            for c in copies:
                c.start()

    hop_mark = take(8)

    def hops(k):
        sec = rsec(xm if k % 2 == 0 else xp, *order[k])
        to = xright if k % 2 == 0 else xleft
        return (sec, describe(hop_mark + 2 * k, rtiles(sec), rtiles(sec), rr.at[sec], to),
                describe(hop_mark + 2 * k + 1, rmv.at[sec], rmv.at[sec], rmr.at[sec], to))

    def hop_on(ks):
        for k in ks:
            sec, a, b = hops(k)
            rarrive(sec)
            a.start()
            b.start()

    no_base = jnp.logical_not(is_base)
    differs = jnp.logical_not(same)

    def last_right():
        @pl.when(is_base)
        def _():
            for k in range(4):
                rarrive(rsec((x + 2) % NX, *order[k]))

        @pl.when(no_base)
        def _():
            for k in range(4):
                rarrive(rsec(xp if k % 2 == 0 else xm, *order[k]))

    def pair_on():
        for h in range(2):
            larrive(pair, h)
            for c in pair_copies(h):
                c.start()

    pair = lslot(y, core, 1 - zp)
    pair_mark = take(12)

    def pair_copies(h):
        i = pair_mark + 6 * h
        for to in (up, down, sibling):
            yield describe(i, ltiles(pair, h), ltiles(pair, h), lr.at[pair, h], to)
            if h == 0:
                yield describe(i + 1, lmv.at[pair], lmv.at[pair], lmr.at[pair], to)
            i += 2

    @pl.when(keeps_own)
    def _():
        base((1, 2, 3))

    lstep(1, 0)
    lsend_own(z_next)

    @pl.when(jnp.logical_and(no_base, same))
    def _():
        hop_on((0, 1))

    lstep(2, 0)

    @pl.when(jnp.logical_and(no_base, same))
    def _():
        hop_on((2, 3))

    @pl.when(jnp.logical_and(is_base, differs))
    def _():
        base((0, 1, 2, 3))

    lstep(3, 0)
    pair_on()

    @pl.when(same)
    def _():
        last_right()

    @pl.when(differs)
    def _():
        @pl.when(no_base)
        def _():
            hop_on((0, 1))
        lstep(1, 1)

        @pl.when(no_base)
        def _():
            hop_on((2, 3))
        lstep(2, 1)
        lstep(3, 1)
        last_right()

    rm_copy = pltpu.make_async_copy(rmv, rms, msem.at[0])
    rm_copy.start()
    om_copy = pltpu.make_async_copy(meta_ref, oms, msem.at[3])
    om_copy.start()

    def widen(sec, carry):
        for i in range(NT):
            rtab[sec * SEC + NT + i] = swap(rtab[sec * SEC + i])
        return carry

    lax.fori_loop(0, 8, widen, 0)

    lane = lax.broadcasted_iota(jnp.int32, (BS, TW), 1)
    low = lane < BS

    def group_of(n):
        away = (n + 1) // 2
        return (y + jnp.where(n % 2 == 1, NY - away, away)) % NY

    def meta_copy(n):
        g = group_of(n)
        return pltpu.make_async_copy(lmv.at[pl.ds(g * 4, 4)], lms.at[pl.ds(g * 4, 4)], msem.at[1 + n % 2])

    def meta_in(n):
        g = group_of(n)
        for q in range(2):
            slot = lslot(g, other, q)
            arrive(lmv.at[slot], lmr.at[slot])
        meta_copy(n).start()

    def compute(n):
        g = group_of(n)
        for q in range(2):
            slot = lslot(g, other, q)
            for h in range(2):
                arrive(ltiles(slot, h), lr.at[slot, h])
        dests = (zl, zf)
        for rb in range(RB):
            tiles = [lbuf[(g * 4 + t) * NT + rb * 3 + p] for t in range(4) for p in range(3)]
            lhs = jnp.concatenate(tiles, axis=1)
            keys = [lms[g * 4 + t, 4 + rb, 64 + s] for t in range(4) for s in range(SLOT)]
            for i, d in enumerate(dests):
                at = (2 * d + core) * 16 + y * 2
                j0 = lms[g * 4, rb, at] + 4
                j1 = lms[g * 4, rb, at + 1] + 4
                for t in range(4):
                    sec = d // 2 * 4 + t
                    for s in range(SLOT):
                        k = keys[t * SLOT + s]
                        lo = rtab[sec * SEC + rms[sec, j0, k]]
                        hi = rtab[sec * SEC + rms[sec, j1, k + 32]]
                        wbuf[rb % 2, pl.ds((t * SLOT + s) * BS, BS), pl.ds(i * TW, TW)] = jnp.where(low, lo, hi)
            res = jnp.dot(lhs, wbuf[rb % 2], preferred_element_type=jnp.float32)
            keep[n, pl.ds(rb * BS, BS), :] = res[:, :TW]
            sbuf[n, pl.ds(rb * BS, BS), :] = res[:, TW:].astype(jnp.bfloat16)

    def zcopy(n):
        return pltpu.make_async_remote_copy(
            src_ref=sbuf.at[n], dst_ref=rbuf.at[n], send_sem=zs.at[n], recv_sem=zr.at[n],
            device_id=z_far, device_id_type=MESH)

    def ycopy(n):
        return pltpu.make_async_remote_copy(
            src_ref=ysend.at[n], dst_ref=yrecv.at[y], send_sem=ys.at[n], recv_sem=yr.at[y],
            device_id=dev(rep, row, group_of(n)), device_id_type=MESH)

    def finish(n):
        arrive(rbuf.at[n], zr.at[n])
        total = (keep[n] + rbuf[n].astype(jnp.float32)).astype(jnp.bfloat16)

        @pl.when(n == 0)
        def _():
            yrecv[y] = total

        @pl.when(n > 0)
        def _():
            ysend[n] = total
            ycopy(n).start()

    par = lax.broadcasted_iota(jnp.int32, (BS, TW), 0) % 2
    half_of = lane // BS

    def combine(s):
        c = group_of(s)

        @pl.when(s > 0)
        def _():
            arrive(yrecv.at[c], yr.at[c])

        for rb in range(RB):
            at = rep * 16 + c * 2
            k0 = c * RB + oms[rb, at]
            k1 = 32 + c * RB + oms[rb, at + 1]
            mine = jnp.where(low, otab[oms[4 + rb, k0]].astype(jnp.float32),
                             otab[oms[4 + rb, k1]].astype(jnp.float32))
            m = 2.0 * mine - yrecv[c, pl.ds(rb * BS, BS), :].astype(jnp.float32)
            turned = pltpu.roll(m, BS, 1)
            out_ref[rb * NY + c] = jnp.where(
                par == half_of, m,
                jnp.where(par == 0, pltpu.roll(turned, BS - 1, 0), pltpu.roll(turned, 1, 0)))

    meta_in(0)
    rm_copy.wait()
    om_copy.wait()

    def main(n, carry):
        @pl.when(n < NY)
        def _():
            for s in range(1, 4):
                @pl.when(jnp.logical_and(n == 2 * s - 1, same))
                def _(s=s):
                    lstep(s, 1)

            @pl.when(n == jnp.where(same, 7, 1))
            def _():
                lstep(4)

            @pl.when(n % 2 == 1)
            def _():
                meta_in(n)

                @pl.when(n < NY - 1)
                def _():
                    meta_in(n + 1)

            meta_copy(n).wait()
            compute(n)
            zcopy(n).start()

        @pl.when(jnp.logical_and(n >= LAG, n < NY + LAG))
        def _():
            finish(n - LAG)

        @pl.when(n >= 2 * LAG)
        def _():
            combine(n - 2 * LAG)
        return carry

    lax.fori_loop(0, NY + 2 * LAG, main, 0)

    for c in sent:
        describe(*c).wait_send()
    for h in range(2):
        for c in pair_copies(h):
            c.wait_send()
    for s in range(1, 5):
        for h, slot, copies in lring(s):
            for c in copies:
                c.wait_send()

    @pl.when(jnp.logical_not(keeps_own))
    def _():
        for c in near_copies():
            c.wait_send()

    @pl.when(is_base)
    def _():
        for k in range(4):
            for c in xcopies(k):
                c.wait_send()

    @pl.when(jnp.logical_not(is_base))
    def _():
        for k in range(4):
            sec, a, b = hops(k)
            a.wait_send()
            b.wait_send()

    def drain(n, carry):
        zcopy(n).wait_send()

        @pl.when(n > 0)
        def _():
            ycopy(n).wait_send()
        return carry

    lax.fori_loop(0, NY, drain, 0)


def local(p_vals, p_cols, f_cols):
    vals = p_vals.reshape(RB, 3, 2, BS, BS)
    left = vals.transpose(0, 1, 3, 2, 4).reshape(NT, BS, TW)
    right = vals.transpose(0, 1, 4, 2, 3).reshape(NT, BS, TW)
    keys = p_cols[:, 0]
    slot = jnp.arange(SLOT, dtype=jnp.int32)[None]
    place = jnp.arange(RB, dtype=jnp.int32)[:, None] * 3 + slot // 2
    hit = keys[:, None, :] == jnp.arange(32, dtype=jnp.int32)[None, :, None]
    lo = jnp.min(jnp.where(hit, (place + slot % 2 * NT)[:, None], 2 * NT), axis=2)
    hi = jnp.min(jnp.where(hit, (place + (1 - slot % 2) * NT)[:, None], 2 * NT), axis=2)
    row_data = jnp.concatenate([lo, hi, jnp.pad(keys, ((0, 0), (0, 64 - SLOT)))], axis=1)
    meta = jnp.concatenate([f_cols.reshape(RB, 128), row_data], axis=0)

    vm = pl.BlockSpec(memory_space=pltpu.VMEM)
    bf, f32 = jnp.bfloat16, jnp.float32
    out = pl.pallas_call(
        kernel,
        out_shape=jax.ShapeDtypeStruct((RB * NY, BS, TW), f32),
        in_specs=[vm] * 3,
        out_specs=vm,
        scratch_shapes=[
            pltpu.VMEM((4 * NY * NT, BS, TW), bf),
            pltpu.VMEM((8 * SEC, BS, TW), bf),
            pltpu.VMEM((SEC, BS, TW), bf),
            pltpu.VMEM((4 * NY, 8, 128), jnp.int32),
            pltpu.VMEM((8, 8, 128), jnp.int32),
            pltpu.SMEM((4 * NY, 8, 128), jnp.int32),
            pltpu.SMEM((8, 8, 128), jnp.int32),
            pltpu.SMEM((8, 128), jnp.int32),
            pltpu.VMEM((2, 4 * SLOT * BS, 2 * TW), bf),
            pltpu.VMEM((NY, RB * BS, TW), f32),
            pltpu.VMEM((NY, RB * BS, TW), bf),
            pltpu.VMEM((NY, RB * BS, TW), bf),
            pltpu.VMEM((NY, RB * BS, TW), bf),
            pltpu.VMEM((NY, RB * BS, TW), bf),
            pltpu.SemaphoreType.DMA((176,)),
            pltpu.SemaphoreType.DMA((4 * NY, 2)),
            pltpu.SemaphoreType.DMA((4 * NY,)),
            pltpu.SemaphoreType.DMA((8,)),
            pltpu.SemaphoreType.DMA((8,)),
            pltpu.SemaphoreType.DMA((NY,)),
            pltpu.SemaphoreType.DMA((NY,)),
            pltpu.SemaphoreType.DMA((NY,)),
            pltpu.SemaphoreType.DMA((NY,)),
            pltpu.SemaphoreType.DMA((4,)),
        ],
        compiler_params=pltpu.CompilerParams(
            collective_id=0, has_side_effects=True, vmem_limit_bytes=48 * 1024 * 1024),
    )(left, right, meta)
    out = out.reshape(RB, NY, BS // 2, 2, TW).transpose(0, 1, 3, 2, 4)
    return out.reshape(RB, 1, NY, 2, BS * BS)


def solution(mesh):
    return jax.shard_map(
        local,
        mesh=mesh,
        in_specs=(
            P(("row", "col"), "rep", None, None),
            P(("row", "col"), "rep", None),
            P(("row", "col"), None, None, None),
        ),
        out_specs=P(("row", "col"), "rep", None, None, None),
        check_vma=False,
    )
```

```python
import functools

import jax
import jax.numpy as jnp
from jax import lax
from jax.experimental import pallas as pl
from jax.experimental.pallas import tpu as pltpu
from jax.sharding import PartitionSpec as P

MESH = pl.DeviceIdType.MESH
BS = 64
TW = 2 * BS
NT = 12
SEC = 25
NX = 4
NZ = 4
NY = 8
RB = 4
SLOT = 6
LAG = 3


def kernel(left_ref, right_ref, meta_ref, out_ref,
           lbuf, rtab, otab, lmv, rmv, lms, rms, oms, wbuf, keep, sbuf, rbuf, ysend, yrecv,
           ssem, lr, lmr, rr, rmr, zs, zr, ys, yr, msem):
    rep = lax.axis_index("rep")
    row = lax.axis_index("row")
    y = lax.axis_index("col")
    core = rep % 2
    zl = rep // 2
    zh = row % 2
    x = row // 2
    zp = zl % 2
    other = 1 - core
    zn = zl + 1 - 2 * zp
    zf = (zl + 2) % NZ
    far_row = row + 1 - 2 * zh
    is_base = x % 2 == zp
    same = core == zh
    keeps_own = jnp.logical_and(is_base, same)

    def dev(a, b, c):
        return {"rep": a, "row": b, "col": c}

    xp = (x + 1) % NX
    xm = (x + NX - 1) % NX
    up, down = dev(rep, row, (y + 1) % NY), dev(rep, row, (y + NY - 1) % NY)
    sibling = dev(zl * 2 + other, row, y)
    z_next = dev(zn * 2 + core, row, y)
    z_far = dev(zf * 2 + core, row, y)
    xright, xleft = dev(rep, xp * 2 + zh, y), dev(rep, xm * 2 + zh, y)

    partners = [xright, xleft, z_far]
    for r in (row, far_row):
        for z in (zl, zn):
            for c in (core, other):
                if not (r is row and z is zl and c is core):
                    partners.append(dev(z * 2 + c, r, y))
    partners += [dev(rep, row, (y + s) % NY) for s in range(1, NY)]
    barrier = pltpu.get_barrier_semaphore()
    for p in partners:
        pl.semaphore_signal(barrier, inc=1, device_id=p, device_id_type=MESH)
    pl.semaphore_wait(barrier, len(partners))

    counter = [0]
    sent = []

    def describe(i, src, dst, rsem, to):
        return pltpu.make_async_remote_copy(
            src_ref=src, dst_ref=dst, send_sem=ssem.at[i], recv_sem=rsem,
            device_id=to, device_id_type=MESH)

    def take(count):
        first = counter[0]
        counter[0] += count
        return first

    def send(src, dst, rsem, to):
        i = take(1)
        describe(i, src, dst, rsem, to).start()
        sent.append((i, src, dst, rsem, to))

    def arrive(dst, rsem):
        pltpu.make_async_remote_copy(
            src_ref=dst, dst_ref=dst, send_sem=ssem.at[0], recv_sem=rsem,
            device_id=sibling, device_id_type=MESH).wait_recv()

    def lslot(yy, c, q):
        return (yy * 2 + c) * 2 + q

    def ltiles(s, h):
        return lbuf.at[pl.ds(s * NT + h * (NT // 2), NT // 2)]

    def rtiles(s):
        return rtab.at[pl.ds(s * SEC, NT)]

    def rsec(xx, c, q):
        return xx // 2 * 4 + c * 2 + q

    own = lslot(y, core, zp)
    own_sec = rsec(x, core, zp)
    zt = jnp.where(is_base, zl, zn)
    base_far = dev(zt * 2 + zh, far_row, y)
    base_near = dev(zt * 2 + zh, row, y)
    near_mark = take(2)

    def near_copies():
        return (describe(near_mark, right_ref, rtiles(own_sec), rr.at[own_sec], base_near),
                describe(near_mark + 1, meta_ref, rmv.at[own_sec], rmr.at[own_sec], base_near))

    send(right_ref, rtiles(own_sec), rr.at[own_sec], base_far)
    send(meta_ref, rmv.at[own_sec], rmr.at[own_sec], base_far)

    @pl.when(jnp.logical_not(keeps_own))
    def _():
        for c in near_copies():
            c.start()

    def lsend_own(to):
        for h in range(2):
            send(left_ref.at[pl.ds(h * (NT // 2), NT // 2)], ltiles(own, h), lr.at[own, h], to)
            if h == 0:
                send(meta_ref, lmv.at[own], lmr.at[own], to)

    for to in (up, down, sibling):
        lsend_own(to)

    order = [(core, zp), (other, zp), (core, 1 - zp), (other, 1 - zp)]
    base_mark = take(16)

    def xcopies(k):
        sec = rsec(x, *order[k])
        i = base_mark + 4 * k
        for to in ((xright, xleft) if k % 2 == 0 else (xleft, xright)):
            yield describe(i, rtiles(sec), rtiles(sec), rr.at[sec], to)
            yield describe(i + 1, rmv.at[sec], rmv.at[sec], rmr.at[sec], to)
            i += 2

    def rarrive(sec):
        arrive(rtiles(sec), rr.at[sec])
        arrive(rmv.at[sec], rmr.at[sec])

    def base(ks):
        for k in ks:
            rarrive(rsec(x, *order[k]))
            for c in xcopies(k):
                c.start()

    @pl.when(keeps_own)
    def _():
        rtab[pl.ds(own_sec * SEC, NT)] = right_ref[...]
        rmv[own_sec] = meta_ref[...]
        for c in xcopies(0):
            c.start()

    lbuf[pl.ds(own * NT, NT)] = left_ref[...]
    lmv[own] = meta_ref[...]
    zero_tile = jnp.zeros((BS, TW), jnp.bfloat16)
    for s in range(8):
        rtab[s * SEC + 2 * NT] = zero_tile
    otab[2 * NT] = zero_tile

    def swap(v):
        return jnp.concatenate([v[:, BS:], v[:, :BS]], axis=1)

    for i in range(NT):
        v = left_ref[i]
        otab[i] = v
        otab[NT + i] = swap(v)

    def larrive(slot, h):
        arrive(ltiles(slot, h), lr.at[slot, h])
        if h == 0:
            arrive(lmv.at[slot], lmr.at[slot])

    marks = {1: take(32), 2: take(32), 3: take(24), 4: take(8)}

    def lring(s, part=None):
        i = marks[s]
        for q, tile in ((zp, 0), (1 - zp, 1)):
            for h in range(2):
                for yy, to, way in (((y + NY - s) % NY, up, 0), ((y + s) % NY, down, 1)):
                    if s == 4 and way != h:
                        continue
                    slot = lslot(yy, core, q)
                    goals = [to] if s < 3 or (s == 3 and h == way) else []
                    copies = []
                    for goal in goals + [sibling]:
                        if part is None or tile == part:
                            copies.append(describe(i, ltiles(slot, h), ltiles(slot, h), lr.at[slot, h], goal))
                            if h == 0:
                                copies.append(describe(i + 1, lmv.at[slot], lmv.at[slot], lmr.at[slot], goal))
                        i += 2
                    if copies:
                        yield h, slot, copies

    def lstep(s, part=None):
        for h, slot, copies in lring(s, part):
            larrive(slot, h)
            for c in copies:
                c.start()

    hop_mark = take(8)

    def hops(k):
        sec = rsec(xm if k % 2 == 0 else xp, *order[k])
        to = xright if k % 2 == 0 else xleft
        return (sec, describe(hop_mark + 2 * k, rtiles(sec), rtiles(sec), rr.at[sec], to),
                describe(hop_mark + 2 * k + 1, rmv.at[sec], rmv.at[sec], rmr.at[sec], to))

    def hop_on(ks):
        for k in ks:
            sec, a, b = hops(k)
            rarrive(sec)
            a.start()
            b.start()

    no_base = jnp.logical_not(is_base)
    differs = jnp.logical_not(same)

    def last_right():
        @pl.when(is_base)
        def _():
            for k in range(4):
                rarrive(rsec((x + 2) % NX, *order[k]))

        @pl.when(no_base)
        def _():
            for k in range(4):
                rarrive(rsec(xp if k % 2 == 0 else xm, *order[k]))

    def pair_on():
        for h in range(2):
            larrive(pair, h)
            for c in pair_copies(h):
                c.start()

    pair = lslot(y, core, 1 - zp)
    pair_mark = take(12)

    def pair_copies(h):
        i = pair_mark + 6 * h
        for to in (up, down, sibling):
            yield describe(i, ltiles(pair, h), ltiles(pair, h), lr.at[pair, h], to)
            if h == 0:
                yield describe(i + 1, lmv.at[pair], lmv.at[pair], lmr.at[pair], to)
            i += 2

    @pl.when(keeps_own)
    def _():
        base((1, 2, 3))

    lstep(1, 0)
    lsend_own(z_next)

    @pl.when(jnp.logical_and(no_base, same))
    def _():
        hop_on((0, 1))

    lstep(2, 0)

    @pl.when(jnp.logical_and(no_base, same))
    def _():
        hop_on((2, 3))

    lstep(3, 0)
    pair_on()

    @pl.when(jnp.logical_and(is_base, differs))
    def _():
        base((0, 1, 2, 3))

    @pl.when(same)
    def _():
        last_right()

    @pl.when(differs)
    def _():
        lstep(1, 1)

        @pl.when(no_base)
        def _():
            hop_on((0, 1))
        lstep(2, 1)

        @pl.when(no_base)
        def _():
            hop_on((2, 3))
        lstep(3, 1)
        last_right()

    rm_copy = pltpu.make_async_copy(rmv, rms, msem.at[0])
    rm_copy.start()
    om_copy = pltpu.make_async_copy(meta_ref, oms, msem.at[3])
    om_copy.start()

    def widen(sec, carry):
        for i in range(NT):
            rtab[sec * SEC + NT + i] = swap(rtab[sec * SEC + i])
        return carry

    lax.fori_loop(0, 8, widen, 0)

    lane = lax.broadcasted_iota(jnp.int32, (BS, TW), 1)
    low = lane < BS

    def group_of(n):
        away = (n + 1) // 2
        return (y + jnp.where(n % 2 == 1, NY - away, away)) % NY

    def meta_copy(n):
        g = group_of(n)
        return pltpu.make_async_copy(lmv.at[pl.ds(g * 4, 4)], lms.at[pl.ds(g * 4, 4)], msem.at[1 + n % 2])

    def meta_in(n):
        g = group_of(n)
        for q in range(2):
            slot = lslot(g, other, q)
            arrive(lmv.at[slot], lmr.at[slot])
        meta_copy(n).start()

    def compute(n):
        g = group_of(n)
        for q in range(2):
            slot = lslot(g, other, q)
            for h in range(2):
                arrive(ltiles(slot, h), lr.at[slot, h])
        dests = (zl, zf)
        for rb in range(RB):
            tiles = [lbuf[(g * 4 + t) * NT + rb * 3 + p] for t in range(4) for p in range(3)]
            lhs = jnp.concatenate(tiles, axis=1)
            keys = [lms[g * 4 + t, 4 + rb, 64 + s] for t in range(4) for s in range(SLOT)]
            for i, d in enumerate(dests):
                at = (2 * d + core) * 16 + y * 2
                j0 = lms[g * 4, rb, at] + 4
                j1 = lms[g * 4, rb, at + 1] + 4
                for t in range(4):
                    sec = d // 2 * 4 + t
                    for s in range(SLOT):
                        k = keys[t * SLOT + s]
                        lo = rtab[sec * SEC + rms[sec, j0, k]]
                        hi = rtab[sec * SEC + rms[sec, j1, k + 32]]
                        wbuf[rb % 2, pl.ds((t * SLOT + s) * BS, BS), pl.ds(i * TW, TW)] = jnp.where(low, lo, hi)
            res = jnp.dot(lhs, wbuf[rb % 2], preferred_element_type=jnp.float32)
            keep[n, pl.ds(rb * BS, BS), :] = res[:, :TW]
            sbuf[n, pl.ds(rb * BS, BS), :] = res[:, TW:].astype(jnp.bfloat16)

    def zcopy(n):
        return pltpu.make_async_remote_copy(
            src_ref=sbuf.at[n], dst_ref=rbuf.at[n], send_sem=zs.at[n], recv_sem=zr.at[n],
            device_id=z_far, device_id_type=MESH)

    def ycopy(n):
        return pltpu.make_async_remote_copy(
            src_ref=ysend.at[n], dst_ref=yrecv.at[y], send_sem=ys.at[n], recv_sem=yr.at[y],
            device_id=dev(rep, row, group_of(n)), device_id_type=MESH)

    def finish(n):
        arrive(rbuf.at[n], zr.at[n])
        total = (keep[n] + rbuf[n].astype(jnp.float32)).astype(jnp.bfloat16)

        @pl.when(n == 0)
        def _():
            yrecv[y] = total

        @pl.when(n > 0)
        def _():
            ysend[n] = total
            ycopy(n).start()

    par = lax.broadcasted_iota(jnp.int32, (BS, TW), 0) % 2
    half_of = lane // BS

    def combine(s):
        c = group_of(s)

        @pl.when(s > 0)
        def _():
            arrive(yrecv.at[c], yr.at[c])

        for rb in range(RB):
            at = rep * 16 + c * 2
            k0 = c * RB + oms[rb, at]
            k1 = 32 + c * RB + oms[rb, at + 1]
            mine = jnp.where(low, otab[oms[4 + rb, k0]].astype(jnp.float32),
                             otab[oms[4 + rb, k1]].astype(jnp.float32))
            m = 2.0 * mine - yrecv[c, pl.ds(rb * BS, BS), :].astype(jnp.float32)
            turned = pltpu.roll(m, BS, 1)
            out_ref[rb * NY + c] = jnp.where(
                par == half_of, m,
                jnp.where(par == 0, pltpu.roll(turned, BS - 1, 0), pltpu.roll(turned, 1, 0)))

    meta_in(0)
    rm_copy.wait()
    om_copy.wait()

    def main(n, carry):
        @pl.when(n < NY)
        def _():
            for s in range(1, 4):
                @pl.when(jnp.logical_and(n == 2 * s - 1, same))
                def _(s=s):
                    lstep(s, 1)

            @pl.when(n == jnp.where(same, 7, 1))
            def _():
                lstep(4)

            @pl.when(n % 2 == 1)
            def _():
                meta_in(n)

                @pl.when(n < NY - 1)
                def _():
                    meta_in(n + 1)

            meta_copy(n).wait()
            compute(n)
            zcopy(n).start()

        @pl.when(jnp.logical_and(n >= LAG, n < NY + LAG))
        def _():
            finish(n - LAG)

        @pl.when(n >= 2 * LAG)
        def _():
            combine(n - 2 * LAG)
        return carry

    lax.fori_loop(0, NY + 2 * LAG, main, 0)

    for c in sent:
        describe(*c).wait_send()
    for h in range(2):
        for c in pair_copies(h):
            c.wait_send()
    for s in range(1, 5):
        for h, slot, copies in lring(s):
            for c in copies:
                c.wait_send()

    @pl.when(jnp.logical_not(keeps_own))
    def _():
        for c in near_copies():
            c.wait_send()

    @pl.when(is_base)
    def _():
        for k in range(4):
            for c in xcopies(k):
                c.wait_send()

    @pl.when(jnp.logical_not(is_base))
    def _():
        for k in range(4):
            sec, a, b = hops(k)
            a.wait_send()
            b.wait_send()

    def drain(n, carry):
        zcopy(n).wait_send()

        @pl.when(n > 0)
        def _():
            ycopy(n).wait_send()
        return carry

    lax.fori_loop(0, NY, drain, 0)


def local(p_vals, p_cols, f_cols):
    vals = p_vals.reshape(RB, 3, 2, BS, BS)
    left = vals.transpose(0, 1, 3, 2, 4).reshape(NT, BS, TW)
    right = vals.transpose(0, 1, 4, 2, 3).reshape(NT, BS, TW)
    keys = p_cols[:, 0]
    slot = jnp.arange(SLOT, dtype=jnp.int32)[None]
    place = jnp.arange(RB, dtype=jnp.int32)[:, None] * 3 + slot // 2
    hit = keys[:, None, :] == jnp.arange(32, dtype=jnp.int32)[None, :, None]
    lo = jnp.min(jnp.where(hit, (place + slot % 2 * NT)[:, None], 2 * NT), axis=2)
    hi = jnp.min(jnp.where(hit, (place + (1 - slot % 2) * NT)[:, None], 2 * NT), axis=2)
    row_data = jnp.concatenate([lo, hi, jnp.pad(keys, ((0, 0), (0, 64 - SLOT)))], axis=1)
    meta = jnp.concatenate([f_cols.reshape(RB, 128), row_data], axis=0)

    vm = pl.BlockSpec(memory_space=pltpu.VMEM)
    bf, f32 = jnp.bfloat16, jnp.float32
    out = pl.pallas_call(
        kernel,
        out_shape=jax.ShapeDtypeStruct((RB * NY, BS, TW), f32),
        in_specs=[vm] * 3,
        out_specs=vm,
        scratch_shapes=[
            pltpu.VMEM((4 * NY * NT, BS, TW), bf),
            pltpu.VMEM((8 * SEC, BS, TW), bf),
            pltpu.VMEM((SEC, BS, TW), bf),
            pltpu.VMEM((4 * NY, 8, 128), jnp.int32),
            pltpu.VMEM((8, 8, 128), jnp.int32),
            pltpu.SMEM((4 * NY, 8, 128), jnp.int32),
            pltpu.SMEM((8, 8, 128), jnp.int32),
            pltpu.SMEM((8, 128), jnp.int32),
            pltpu.VMEM((2, 4 * SLOT * BS, 2 * TW), bf),
            pltpu.VMEM((NY, RB * BS, TW), f32),
            pltpu.VMEM((NY, RB * BS, TW), bf),
            pltpu.VMEM((NY, RB * BS, TW), bf),
            pltpu.VMEM((NY, RB * BS, TW), bf),
            pltpu.VMEM((NY, RB * BS, TW), bf),
            pltpu.SemaphoreType.DMA((176,)),
            pltpu.SemaphoreType.DMA((4 * NY, 2)),
            pltpu.SemaphoreType.DMA((4 * NY,)),
            pltpu.SemaphoreType.DMA((8,)),
            pltpu.SemaphoreType.DMA((8,)),
            pltpu.SemaphoreType.DMA((NY,)),
            pltpu.SemaphoreType.DMA((NY,)),
            pltpu.SemaphoreType.DMA((NY,)),
            pltpu.SemaphoreType.DMA((NY,)),
            pltpu.SemaphoreType.DMA((4,)),
        ],
        compiler_params=pltpu.CompilerParams(
            collective_id=0, has_side_effects=True, vmem_limit_bytes=48 * 1024 * 1024),
    )(left, right, meta)
    out = out.reshape(RB, NY, BS // 2, 2, TW).transpose(0, 1, 3, 2, 4)
    return out.reshape(RB, 1, NY, 2, BS * BS)


def solution(mesh):
    return jax.shard_map(
        local,
        mesh=mesh,
        in_specs=(
            P(("row", "col"), "rep", None, None),
            P(("row", "col"), "rep", None),
            P(("row", "col"), None, None, None),
        ),
        out_specs=P(("row", "col"), "rep", None, None, None),
        check_vma=False,
    )
```

```python
import functools

import jax
import jax.numpy as jnp
from jax import lax
from jax.experimental import pallas as pl
from jax.experimental.pallas import tpu as pltpu
from jax.sharding import PartitionSpec as P

MESH = pl.DeviceIdType.MESH
BS = 64
TW = 2 * BS
NT = 12
SEC = 25
NX = 4
NZ = 4
NY = 8
RB = 4
SLOT = 6
LAG = 4


def kernel(left_ref, right_ref, meta_ref, out_ref,
           lbuf, rtab, otab, lmv, rmv, lms, rms, oms, wbuf, keep, sbuf, rbuf, ysend, yrecv,
           ssem, lr, lmr, rr, rmr, zs, zr, ys, yr, msem):
    rep = lax.axis_index("rep")
    row = lax.axis_index("row")
    y = lax.axis_index("col")
    core = rep % 2
    zl = rep // 2
    zh = row % 2
    x = row // 2
    zp = zl % 2
    other = 1 - core
    zn = zl + 1 - 2 * zp
    zf = (zl + 2) % NZ
    far_row = row + 1 - 2 * zh
    is_base = x % 2 == zp
    same = core == zh
    keeps_own = jnp.logical_and(is_base, same)

    def dev(a, b, c):
        return {"rep": a, "row": b, "col": c}

    xp = (x + 1) % NX
    xm = (x + NX - 1) % NX
    up, down = dev(rep, row, (y + 1) % NY), dev(rep, row, (y + NY - 1) % NY)
    sibling = dev(zl * 2 + other, row, y)
    z_next = dev(zn * 2 + core, row, y)
    z_far = dev(zf * 2 + core, row, y)
    xright, xleft = dev(rep, xp * 2 + zh, y), dev(rep, xm * 2 + zh, y)

    partners = [xright, xleft, z_far]
    for r in (row, far_row):
        for z in (zl, zn):
            for c in (core, other):
                if not (r is row and z is zl and c is core):
                    partners.append(dev(z * 2 + c, r, y))
    partners += [dev(rep, row, (y + s) % NY) for s in range(1, NY)]
    barrier = pltpu.get_barrier_semaphore()
    for p in partners:
        pl.semaphore_signal(barrier, inc=1, device_id=p, device_id_type=MESH)
    pl.semaphore_wait(barrier, len(partners))

    counter = [0]
    sent = []

    def describe(i, src, dst, rsem, to):
        return pltpu.make_async_remote_copy(
            src_ref=src, dst_ref=dst, send_sem=ssem.at[i], recv_sem=rsem,
            device_id=to, device_id_type=MESH)

    def take(count):
        first = counter[0]
        counter[0] += count
        return first

    def send(src, dst, rsem, to):
        i = take(1)
        describe(i, src, dst, rsem, to).start()
        sent.append((i, src, dst, rsem, to))

    def arrive(dst, rsem):
        pltpu.make_async_remote_copy(
            src_ref=dst, dst_ref=dst, send_sem=ssem.at[0], recv_sem=rsem,
            device_id=sibling, device_id_type=MESH).wait_recv()

    def lslot(yy, c, q):
        return (yy * 2 + c) * 2 + q

    def ltiles(s, h):
        return lbuf.at[pl.ds(s * NT + h * (NT // 2), NT // 2)]

    def rtiles(s):
        return rtab.at[pl.ds(s * SEC, NT)]

    def rsec(xx, c, q):
        return xx // 2 * 4 + c * 2 + q

    own = lslot(y, core, zp)
    own_sec = rsec(x, core, zp)
    zt = jnp.where(is_base, zl, zn)
    base_far = dev(zt * 2 + zh, far_row, y)
    base_near = dev(zt * 2 + zh, row, y)
    near_mark = take(2)

    def near_copies():
        return (describe(near_mark, right_ref, rtiles(own_sec), rr.at[own_sec], base_near),
                describe(near_mark + 1, meta_ref, rmv.at[own_sec], rmr.at[own_sec], base_near))

    send(right_ref, rtiles(own_sec), rr.at[own_sec], base_far)
    send(meta_ref, rmv.at[own_sec], rmr.at[own_sec], base_far)

    @pl.when(jnp.logical_not(keeps_own))
    def _():
        for c in near_copies():
            c.start()

    def lsend_own(to):
        for h in range(2):
            send(left_ref.at[pl.ds(h * (NT // 2), NT // 2)], ltiles(own, h), lr.at[own, h], to)
            if h == 0:
                send(meta_ref, lmv.at[own], lmr.at[own], to)

    for to in (up, down, sibling):
        lsend_own(to)

    order = [(core, zp), (other, zp), (core, 1 - zp), (other, 1 - zp)]
    base_mark = take(16)

    def xcopies(k):
        sec = rsec(x, *order[k])
        i = base_mark + 4 * k
        for to in ((xright, xleft) if k % 2 == 0 else (xleft, xright)):
            yield describe(i, rtiles(sec), rtiles(sec), rr.at[sec], to)
            yield describe(i + 1, rmv.at[sec], rmv.at[sec], rmr.at[sec], to)
            i += 2

    def rarrive(sec):
        arrive(rtiles(sec), rr.at[sec])
        arrive(rmv.at[sec], rmr.at[sec])

    def base(ks):
        for k in ks:
            rarrive(rsec(x, *order[k]))
            for c in xcopies(k):
                c.start()

    @pl.when(keeps_own)
    def _():
        rtab[pl.ds(own_sec * SEC, NT)] = right_ref[...]
        rmv[own_sec] = meta_ref[...]
        for c in xcopies(0):
            c.start()

    lbuf[pl.ds(own * NT, NT)] = left_ref[...]
    lmv[own] = meta_ref[...]
    zero_tile = jnp.zeros((BS, TW), jnp.bfloat16)
    for s in range(8):
        rtab[s * SEC + 2 * NT] = zero_tile
    otab[2 * NT] = zero_tile

    def swap(v):
        return jnp.concatenate([v[:, BS:], v[:, :BS]], axis=1)

    for i in range(NT):
        v = left_ref[i]
        otab[i] = v
        otab[NT + i] = swap(v)

    def larrive(slot, h):
        arrive(ltiles(slot, h), lr.at[slot, h])
        if h == 0:
            arrive(lmv.at[slot], lmr.at[slot])

    marks = {1: take(32), 2: take(32), 3: take(24), 4: take(8)}

    def lring(s, part=None):
        i = marks[s]
        for q, tile in ((zp, 0), (1 - zp, 1)):
            for h in range(2):
                for yy, to, way in (((y + NY - s) % NY, up, 0), ((y + s) % NY, down, 1)):
                    if s == 4 and way != h:
                        continue
                    slot = lslot(yy, core, q)
                    goals = [to] if s < 3 or (s == 3 and h == way) else []
                    copies = []
                    for goal in goals + [sibling]:
                        if part is None or tile == part:
                            copies.append(describe(i, ltiles(slot, h), ltiles(slot, h), lr.at[slot, h], goal))
                            if h == 0:
                                copies.append(describe(i + 1, lmv.at[slot], lmv.at[slot], lmr.at[slot], goal))
                        i += 2
                    if copies:
                        yield h, slot, copies

    def lstep(s, part=None):
        for h, slot, copies in lring(s, part):
            larrive(slot, h)
            for c in copies:
                c.start()

    hop_mark = take(8)

    def hops(k):
        sec = rsec(xm if k % 2 == 0 else xp, *order[k])
        to = xright if k % 2 == 0 else xleft
        return (sec, describe(hop_mark + 2 * k, rtiles(sec), rtiles(sec), rr.at[sec], to),
                describe(hop_mark + 2 * k + 1, rmv.at[sec], rmv.at[sec], rmr.at[sec], to))

    def hop_on(ks):
        for k in ks:
            sec, a, b = hops(k)
            rarrive(sec)
            a.start()
            b.start()

    no_base = jnp.logical_not(is_base)
    differs = jnp.logical_not(same)

    def last_right():
        @pl.when(is_base)
        def _():
            for k in range(4):
                rarrive(rsec((x + 2) % NX, *order[k]))

        @pl.when(no_base)
        def _():
            for k in range(4):
                rarrive(rsec(xp if k % 2 == 0 else xm, *order[k]))

    def pair_on():
        for h in range(2):
            larrive(pair, h)
            for c in pair_copies(h):
                c.start()

    pair = lslot(y, core, 1 - zp)
    pair_mark = take(12)

    def pair_copies(h):
        i = pair_mark + 6 * h
        for to in (up, down, sibling):
            yield describe(i, ltiles(pair, h), ltiles(pair, h), lr.at[pair, h], to)
            if h == 0:
                yield describe(i + 1, lmv.at[pair], lmv.at[pair], lmr.at[pair], to)
            i += 2

    @pl.when(keeps_own)
    def _():
        base((1, 2, 3))

    lstep(1, 0)
    lsend_own(z_next)

    @pl.when(jnp.logical_and(no_base, same))
    def _():
        hop_on((0, 1))

    lstep(2, 0)

    @pl.when(jnp.logical_and(no_base, same))
    def _():
        hop_on((2, 3))

    lstep(3, 0)
    pair_on()

    @pl.when(jnp.logical_and(is_base, differs))
    def _():
        base((0, 1, 2, 3))

    @pl.when(same)
    def _():
        last_right()

    @pl.when(differs)
    def _():
        lstep(1, 1)

        @pl.when(no_base)
        def _():
            hop_on((0, 1))
        lstep(2, 1)

        @pl.when(no_base)
        def _():
            hop_on((2, 3))
        lstep(3, 1)
        last_right()

    rm_copy = pltpu.make_async_copy(rmv, rms, msem.at[0])
    rm_copy.start()
    om_copy = pltpu.make_async_copy(meta_ref, oms, msem.at[3])
    om_copy.start()

    def widen(sec, carry):
        for i in range(NT):
            rtab[sec * SEC + NT + i] = swap(rtab[sec * SEC + i])
        return carry

    lax.fori_loop(0, 8, widen, 0)

    lane = lax.broadcasted_iota(jnp.int32, (BS, TW), 1)
    low = lane < BS

    def group_of(n):
        away = (n + 1) // 2
        return (y + jnp.where(n % 2 == 1, NY - away, away)) % NY

    def meta_copy(n):
        g = group_of(n)
        return pltpu.make_async_copy(lmv.at[pl.ds(g * 4, 4)], lms.at[pl.ds(g * 4, 4)], msem.at[1 + n % 2])

    def meta_in(n):
        g = group_of(n)
        for q in range(2):
            slot = lslot(g, other, q)
            arrive(lmv.at[slot], lmr.at[slot])
        meta_copy(n).start()

    def compute(n):
        g = group_of(n)
        for q in range(2):
            slot = lslot(g, other, q)
            for h in range(2):
                arrive(ltiles(slot, h), lr.at[slot, h])
        dests = (zl, zf)
        for rb in range(RB):
            tiles = [lbuf[(g * 4 + t) * NT + rb * 3 + p] for t in range(4) for p in range(3)]
            lhs = jnp.concatenate(tiles, axis=1)
            keys = [lms[g * 4 + t, 4 + rb, 64 + s] for t in range(4) for s in range(SLOT)]
            for i, d in enumerate(dests):
                at = (2 * d + core) * 16 + y * 2
                j0 = lms[g * 4, rb, at] + 4
                j1 = lms[g * 4, rb, at + 1] + 4
                for t in range(4):
                    sec = d // 2 * 4 + t
                    for s in range(SLOT):
                        k = keys[t * SLOT + s]
                        lo = rtab[sec * SEC + rms[sec, j0, k]]
                        hi = rtab[sec * SEC + rms[sec, j1, k + 32]]
                        wbuf[rb % 2, pl.ds((t * SLOT + s) * BS, BS), pl.ds(i * TW, TW)] = jnp.where(low, lo, hi)
            res = jnp.dot(lhs, wbuf[rb % 2], preferred_element_type=jnp.float32)
            keep[n, pl.ds(rb * BS, BS), :] = res[:, :TW]
            sbuf[n, pl.ds(rb * BS, BS), :] = res[:, TW:].astype(jnp.bfloat16)

    def zcopy(n):
        return pltpu.make_async_remote_copy(
            src_ref=sbuf.at[n], dst_ref=rbuf.at[n], send_sem=zs.at[n], recv_sem=zr.at[n],
            device_id=z_far, device_id_type=MESH)

    def ycopy(n):
        return pltpu.make_async_remote_copy(
            src_ref=ysend.at[n], dst_ref=yrecv.at[y], send_sem=ys.at[n], recv_sem=yr.at[y],
            device_id=dev(rep, row, group_of(n)), device_id_type=MESH)

    def finish(n):
        arrive(rbuf.at[n], zr.at[n])
        total = (keep[n] + rbuf[n].astype(jnp.float32)).astype(jnp.bfloat16)

        @pl.when(n == 0)
        def _():
            yrecv[y] = total

        @pl.when(n > 0)
        def _():
            ysend[n] = total
            ycopy(n).start()

    par = lax.broadcasted_iota(jnp.int32, (BS, TW), 0) % 2
    half_of = lane // BS

    def combine(s):
        c = group_of(s)

        @pl.when(s > 0)
        def _():
            arrive(yrecv.at[c], yr.at[c])

        for rb in range(RB):
            at = rep * 16 + c * 2
            k0 = c * RB + oms[rb, at]
            k1 = 32 + c * RB + oms[rb, at + 1]
            mine = jnp.where(low, otab[oms[4 + rb, k0]].astype(jnp.float32),
                             otab[oms[4 + rb, k1]].astype(jnp.float32))
            m = 2.0 * mine - yrecv[c, pl.ds(rb * BS, BS), :].astype(jnp.float32)
            turned = pltpu.roll(m, BS, 1)
            out_ref[rb * NY + c] = jnp.where(
                par == half_of, m,
                jnp.where(par == 0, pltpu.roll(turned, BS - 1, 0), pltpu.roll(turned, 1, 0)))

    meta_in(0)
    rm_copy.wait()
    om_copy.wait()

    def main(n, carry):
        @pl.when(n < NY)
        def _():
            for s in range(1, 4):
                @pl.when(jnp.logical_and(n == 2 * s - 1, same))
                def _(s=s):
                    lstep(s, 1)

            @pl.when(n == jnp.where(same, 7, 1))
            def _():
                lstep(4)

            @pl.when(n % 2 == 1)
            def _():
                meta_in(n)

                @pl.when(n < NY - 1)
                def _():
                    meta_in(n + 1)

            meta_copy(n).wait()
            compute(n)
            zcopy(n).start()

        @pl.when(jnp.logical_and(n >= LAG, n < NY + LAG))
        def _():
            finish(n - LAG)

        @pl.when(n >= 2 * LAG)
        def _():
            combine(n - 2 * LAG)
        return carry

    lax.fori_loop(0, NY + 2 * LAG, main, 0)

    for c in sent:
        describe(*c).wait_send()
    for h in range(2):
        for c in pair_copies(h):
            c.wait_send()
    for s in range(1, 5):
        for h, slot, copies in lring(s):
            for c in copies:
                c.wait_send()

    @pl.when(jnp.logical_not(keeps_own))
    def _():
        for c in near_copies():
            c.wait_send()

    @pl.when(is_base)
    def _():
        for k in range(4):
            for c in xcopies(k):
                c.wait_send()

    @pl.when(jnp.logical_not(is_base))
    def _():
        for k in range(4):
            sec, a, b = hops(k)
            a.wait_send()
            b.wait_send()

    def drain(n, carry):
        zcopy(n).wait_send()

        @pl.when(n > 0)
        def _():
            ycopy(n).wait_send()
        return carry

    lax.fori_loop(0, NY, drain, 0)


def local(p_vals, p_cols, f_cols):
    vals = p_vals.reshape(RB, 3, 2, BS, BS)
    left = vals.transpose(0, 1, 3, 2, 4).reshape(NT, BS, TW)
    right = vals.transpose(0, 1, 4, 2, 3).reshape(NT, BS, TW)
    keys = p_cols[:, 0]
    slot = jnp.arange(SLOT, dtype=jnp.int32)[None]
    place = jnp.arange(RB, dtype=jnp.int32)[:, None] * 3 + slot // 2
    hit = keys[:, None, :] == jnp.arange(32, dtype=jnp.int32)[None, :, None]
    lo = jnp.min(jnp.where(hit, (place + slot % 2 * NT)[:, None], 2 * NT), axis=2)
    hi = jnp.min(jnp.where(hit, (place + (1 - slot % 2) * NT)[:, None], 2 * NT), axis=2)
    row_data = jnp.concatenate([lo, hi, jnp.pad(keys, ((0, 0), (0, 64 - SLOT)))], axis=1)
    meta = jnp.concatenate([f_cols.reshape(RB, 128), row_data], axis=0)

    vm = pl.BlockSpec(memory_space=pltpu.VMEM)
    bf, f32 = jnp.bfloat16, jnp.float32
    out = pl.pallas_call(
        kernel,
        out_shape=jax.ShapeDtypeStruct((RB * NY, BS, TW), f32),
        in_specs=[vm] * 3,
        out_specs=vm,
        scratch_shapes=[
            pltpu.VMEM((4 * NY * NT, BS, TW), bf),
            pltpu.VMEM((8 * SEC, BS, TW), bf),
            pltpu.VMEM((SEC, BS, TW), bf),
            pltpu.VMEM((4 * NY, 8, 128), jnp.int32),
            pltpu.VMEM((8, 8, 128), jnp.int32),
            pltpu.SMEM((4 * NY, 8, 128), jnp.int32),
            pltpu.SMEM((8, 8, 128), jnp.int32),
            pltpu.SMEM((8, 128), jnp.int32),
            pltpu.VMEM((2, 4 * SLOT * BS, 2 * TW), bf),
            pltpu.VMEM((NY, RB * BS, TW), f32),
            pltpu.VMEM((NY, RB * BS, TW), bf),
            pltpu.VMEM((NY, RB * BS, TW), bf),
            pltpu.VMEM((NY, RB * BS, TW), bf),
            pltpu.VMEM((NY, RB * BS, TW), bf),
            pltpu.SemaphoreType.DMA((176,)),
            pltpu.SemaphoreType.DMA((4 * NY, 2)),
            pltpu.SemaphoreType.DMA((4 * NY,)),
            pltpu.SemaphoreType.DMA((8,)),
            pltpu.SemaphoreType.DMA((8,)),
            pltpu.SemaphoreType.DMA((NY,)),
            pltpu.SemaphoreType.DMA((NY,)),
            pltpu.SemaphoreType.DMA((NY,)),
            pltpu.SemaphoreType.DMA((NY,)),
            pltpu.SemaphoreType.DMA((4,)),
        ],
        compiler_params=pltpu.CompilerParams(
            collective_id=0, has_side_effects=True, vmem_limit_bytes=48 * 1024 * 1024),
    )(left, right, meta)
    out = out.reshape(RB, NY, BS // 2, 2, TW).transpose(0, 1, 3, 2, 4)
    return out.reshape(RB, 1, NY, 2, BS * BS)


def solution(mesh):
    return jax.shard_map(
        local,
        mesh=mesh,
        in_specs=(
            P(("row", "col"), "rep", None, None),
            P(("row", "col"), "rep", None),
            P(("row", "col"), None, None, None),
        ),
        out_specs=P(("row", "col"), "rep", None, None, None),
        check_vma=False,
    )
```

```python
import functools

import jax
import jax.numpy as jnp
from jax import lax
from jax.experimental import pallas as pl
from jax.experimental.pallas import tpu as pltpu
from jax.sharding import PartitionSpec as P

MESH = pl.DeviceIdType.MESH
BS = 64
TW = 2 * BS
NT = 12
SEC = 25
NX = 4
NZ = 4
NY = 8
RB = 4
SLOT = 6
LAG = 4


def kernel(left_ref, right_ref, meta_ref, out_ref,
           lbuf, rtab, otab, lmv, rmv, lms, rms, oms, wbuf, keep, sbuf, rbuf, ysend, yrecv,
           ssem, lr, lmr, rr, rmr, zs, zr, ys, yr, msem):
    rep = lax.axis_index("rep")
    row = lax.axis_index("row")
    y = lax.axis_index("col")
    core = rep % 2
    zl = rep // 2
    zh = row % 2
    x = row // 2
    zp = zl % 2
    other = 1 - core
    zn = zl + 1 - 2 * zp
    zf = (zl + 2) % NZ
    far_row = row + 1 - 2 * zh
    is_base = x % 2 == zp
    same = core == zh
    keeps_own = jnp.logical_and(is_base, same)

    def dev(a, b, c):
        return {"rep": a, "row": b, "col": c}

    xp = (x + 1) % NX
    xm = (x + NX - 1) % NX
    up, down = dev(rep, row, (y + 1) % NY), dev(rep, row, (y + NY - 1) % NY)
    sibling = dev(zl * 2 + other, row, y)
    z_next = dev(zn * 2 + core, row, y)
    z_far = dev(zf * 2 + core, row, y)
    xright, xleft = dev(rep, xp * 2 + zh, y), dev(rep, xm * 2 + zh, y)

    partners = [xright, xleft, z_far]
    for r in (row, far_row):
        for z in (zl, zn):
            for c in (core, other):
                if not (r is row and z is zl and c is core):
                    partners.append(dev(z * 2 + c, r, y))
    partners += [dev(rep, row, (y + s) % NY) for s in range(1, NY)]
    barrier = pltpu.get_barrier_semaphore()
    for p in partners:
        pl.semaphore_signal(barrier, inc=1, device_id=p, device_id_type=MESH)
    pl.semaphore_wait(barrier, len(partners))

    counter = [0]
    sent = []

    def describe(i, src, dst, rsem, to):
        return pltpu.make_async_remote_copy(
            src_ref=src, dst_ref=dst, send_sem=ssem.at[i], recv_sem=rsem,
            device_id=to, device_id_type=MESH)

    def take(count):
        first = counter[0]
        counter[0] += count
        return first

    def send(src, dst, rsem, to):
        i = take(1)
        describe(i, src, dst, rsem, to).start()
        sent.append((i, src, dst, rsem, to))

    def arrive(dst, rsem):
        pltpu.make_async_remote_copy(
            src_ref=dst, dst_ref=dst, send_sem=ssem.at[0], recv_sem=rsem,
            device_id=sibling, device_id_type=MESH).wait_recv()

    def lslot(yy, c, q):
        return (yy * 2 + c) * 2 + q

    def ltiles(s, h):
        return lbuf.at[pl.ds(s * NT + h * (NT // 2), NT // 2)]

    def rtiles(s):
        return rtab.at[pl.ds(s * SEC, NT)]

    def rsec(xx, c, q):
        return xx // 2 * 4 + c * 2 + q

    own = lslot(y, core, zp)
    own_sec = rsec(x, core, zp)
    zt = jnp.where(is_base, zl, zn)
    base_far = dev(zt * 2 + zh, far_row, y)
    base_near = dev(zt * 2 + zh, row, y)
    near_mark = take(2)

    def near_copies():
        return (describe(near_mark, right_ref, rtiles(own_sec), rr.at[own_sec], base_near),
                describe(near_mark + 1, meta_ref, rmv.at[own_sec], rmr.at[own_sec], base_near))

    send(right_ref, rtiles(own_sec), rr.at[own_sec], base_far)
    send(meta_ref, rmv.at[own_sec], rmr.at[own_sec], base_far)

    @pl.when(jnp.logical_not(keeps_own))
    def _():
        for c in near_copies():
            c.start()

    def lsend_own(to):
        for h in range(2):
            send(left_ref.at[pl.ds(h * (NT // 2), NT // 2)], ltiles(own, h), lr.at[own, h], to)
            if h == 0:
                send(meta_ref, lmv.at[own], lmr.at[own], to)

    for to in (up, down, sibling):
        lsend_own(to)

    order = [(core, zp), (other, zp), (core, 1 - zp), (other, 1 - zp)]
    base_mark = take(16)

    def xcopies(k):
        sec = rsec(x, *order[k])
        i = base_mark + 4 * k
        for to in ((xright, xleft) if k % 2 == 0 else (xleft, xright)):
            yield describe(i, rtiles(sec), rtiles(sec), rr.at[sec], to)
            yield describe(i + 1, rmv.at[sec], rmv.at[sec], rmr.at[sec], to)
            i += 2

    def rarrive(sec):
        arrive(rtiles(sec), rr.at[sec])
        arrive(rmv.at[sec], rmr.at[sec])

    def base(ks):
        for k in ks:
            rarrive(rsec(x, *order[k]))
            for c in xcopies(k):
                c.start()

    @pl.when(keeps_own)
    def _():
        rtab[pl.ds(own_sec * SEC, NT)] = right_ref[...]
        rmv[own_sec] = meta_ref[...]
        for c in xcopies(0):
            c.start()

    lbuf[pl.ds(own * NT, NT)] = left_ref[...]
    lmv[own] = meta_ref[...]
    zero_tile = jnp.zeros((BS, TW), jnp.bfloat16)
    for s in range(8):
        rtab[s * SEC + 2 * NT] = zero_tile
    otab[2 * NT] = zero_tile

    def swap(v):
        return jnp.concatenate([v[:, BS:], v[:, :BS]], axis=1)

    for i in range(NT):
        v = left_ref[i]
        otab[i] = v
        otab[NT + i] = swap(v)

    def larrive(slot, h):
        arrive(ltiles(slot, h), lr.at[slot, h])
        if h == 0:
            arrive(lmv.at[slot], lmr.at[slot])

    marks = {1: take(32), 2: take(32), 3: take(24), 4: take(8)}

    def lring(s, part=None):
        i = marks[s]
        for q, tile in ((zp, 0), (1 - zp, 1)):
            for h in range(2):
                for yy, to, way in (((y + NY - s) % NY, up, 0), ((y + s) % NY, down, 1)):
                    if s == 4 and way != h:
                        continue
                    slot = lslot(yy, core, q)
                    goals = [to] if s < 3 or (s == 3 and h == way) else []
                    copies = []
                    for goal in goals + [sibling]:
                        if part is None or tile == part:
                            copies.append(describe(i, ltiles(slot, h), ltiles(slot, h), lr.at[slot, h], goal))
                            if h == 0:
                                copies.append(describe(i + 1, lmv.at[slot], lmv.at[slot], lmr.at[slot], goal))
                        i += 2
                    if copies:
                        yield h, slot, copies

    def lstep(s, part=None):
        for h, slot, copies in lring(s, part):
            larrive(slot, h)
            for c in copies:
                c.start()

    hop_mark = take(8)

    def hops(k):
        sec = rsec(xm if k % 2 == 0 else xp, *order[k])
        to = xright if k % 2 == 0 else xleft
        return (sec, describe(hop_mark + 2 * k, rtiles(sec), rtiles(sec), rr.at[sec], to),
                describe(hop_mark + 2 * k + 1, rmv.at[sec], rmv.at[sec], rmr.at[sec], to))

    def hop_on(ks):
        for k in ks:
            sec, a, b = hops(k)
            rarrive(sec)
            a.start()
            b.start()

    no_base = jnp.logical_not(is_base)
    differs = jnp.logical_not(same)

    def last_right():
        @pl.when(is_base)
        def _():
            for k in range(4):
                rarrive(rsec((x + 2) % NX, *order[k]))

        @pl.when(no_base)
        def _():
            for k in range(4):
                rarrive(rsec(xp if k % 2 == 0 else xm, *order[k]))

    def pair_on():
        for h in range(2):
            larrive(pair, h)
            for c in pair_copies(h):
                c.start()

    pair = lslot(y, core, 1 - zp)
    pair_mark = take(12)

    def pair_copies(h):
        i = pair_mark + 6 * h
        for to in (up, down, sibling):
            yield describe(i, ltiles(pair, h), ltiles(pair, h), lr.at[pair, h], to)
            if h == 0:
                yield describe(i + 1, lmv.at[pair], lmv.at[pair], lmr.at[pair], to)
            i += 2

    @pl.when(keeps_own)
    def _():
        base((1, 2, 3))

    lstep(1, 0)
    lsend_own(z_next)

    @pl.when(jnp.logical_and(no_base, same))
    def _():
        hop_on((0, 1))

    lstep(2, 0)

    @pl.when(jnp.logical_and(no_base, same))
    def _():
        hop_on((2, 3))

    lstep(3, 0)
    pair_on()

    @pl.when(jnp.logical_and(is_base, differs))
    def _():
        base((0, 1, 2, 3))

    @pl.when(same)
    def _():
        last_right()

    @pl.when(differs)
    def _():
        lstep(1, 1)

        @pl.when(no_base)
        def _():
            hop_on((0, 1))
        lstep(2, 1)

        @pl.when(no_base)
        def _():
            hop_on((2, 3))
        lstep(3, 1)
        last_right()

    rm_copy = pltpu.make_async_copy(rmv, rms, msem.at[0])
    rm_copy.start()
    om_copy = pltpu.make_async_copy(meta_ref, oms, msem.at[3])
    om_copy.start()

    def widen(sec, carry):
        for i in range(NT):
            rtab[sec * SEC + NT + i] = swap(rtab[sec * SEC + i])
        return carry

    lax.fori_loop(0, 8, widen, 0)

    lane = lax.broadcasted_iota(jnp.int32, (BS, TW), 1)
    low = lane < BS

    def group_of(n):
        away = (n + 1) // 2
        return (y + jnp.where(n % 2 == 1, NY - away, away)) % NY

    def meta_copy(n):
        g = group_of(n)
        return pltpu.make_async_copy(lmv.at[pl.ds(g * 4, 4)], lms.at[pl.ds(g * 4, 4)], msem.at[1 + n % 2])

    def meta_in(n):
        g = group_of(n)
        for q in range(2):
            slot = lslot(g, other, q)
            arrive(lmv.at[slot], lmr.at[slot])
        meta_copy(n).start()

    def compute(n):
        g = group_of(n)
        for q in range(2):
            slot = lslot(g, other, q)
            for h in range(2):
                arrive(ltiles(slot, h), lr.at[slot, h])
        dests = (zl, zf)
        for rb in range(RB):
            tiles = [lbuf[(g * 4 + t) * NT + rb * 3 + p] for t in range(4) for p in range(3)]
            lhs = jnp.concatenate(tiles, axis=1)
            keys = [lms[g * 4 + t, 4 + rb, 64 + s] for t in range(4) for s in range(SLOT)]
            for i, d in enumerate(dests):
                at = (2 * d + core) * 16 + y * 2
                j0 = lms[g * 4, rb, at] + 4
                j1 = lms[g * 4, rb, at + 1] + 4
                for t in range(4):
                    sec = d // 2 * 4 + t
                    for s in range(SLOT):
                        k = keys[t * SLOT + s]
                        lo = rtab[sec * SEC + rms[sec, j0, k]]
                        hi = rtab[sec * SEC + rms[sec, j1, k + 32]]
                        wbuf[rb % 2, pl.ds((t * SLOT + s) * BS, BS), pl.ds(i * TW, TW)] = jnp.where(low, lo, hi)
            res = jnp.dot(lhs, wbuf[rb % 2], preferred_element_type=jnp.float32)
            keep[n, pl.ds(rb * BS, BS), :] = res[:, :TW]
            sbuf[n, pl.ds(rb * BS, BS), :] = res[:, TW:].astype(jnp.bfloat16)

    def zcopy(n):
        return pltpu.make_async_remote_copy(
            src_ref=sbuf.at[n], dst_ref=rbuf.at[n], send_sem=zs.at[n], recv_sem=zr.at[n],
            device_id=z_far, device_id_type=MESH)

    def ycopy(n):
        return pltpu.make_async_remote_copy(
            src_ref=ysend.at[n], dst_ref=yrecv.at[y], send_sem=ys.at[n], recv_sem=yr.at[y],
            device_id=dev(rep, row, group_of(n)), device_id_type=MESH)

    def finish(n):
        arrive(rbuf.at[n], zr.at[n])
        total = (keep[n] + rbuf[n].astype(jnp.float32)).astype(jnp.bfloat16)

        @pl.when(n == 0)
        def _():
            yrecv[y] = total

        @pl.when(n > 0)
        def _():
            ysend[n] = total
            ycopy(n).start()

    par = lax.broadcasted_iota(jnp.int32, (BS, TW), 0) % 2
    half_of = lane // BS

    def combine(s):
        c = group_of(s)

        @pl.when(s > 0)
        def _():
            arrive(yrecv.at[c], yr.at[c])

        for rb in range(RB):
            at = rep * 16 + c * 2
            k0 = c * RB + oms[rb, at]
            k1 = 32 + c * RB + oms[rb, at + 1]
            mine = jnp.where(low, otab[oms[4 + rb, k0]].astype(jnp.float32),
                             otab[oms[4 + rb, k1]].astype(jnp.float32))
            m = 2.0 * mine - yrecv[c, pl.ds(rb * BS, BS), :].astype(jnp.float32)
            turned = pltpu.roll(m, BS, 1)
            out_ref[rb * NY + c] = jnp.where(
                par == half_of, m,
                jnp.where(par == 0, pltpu.roll(turned, BS - 1, 0), pltpu.roll(turned, 1, 0)))

    meta_in(0)
    rm_copy.wait()
    om_copy.wait()

    def main(n, carry):
        @pl.when(n < NY)
        def _():
            for s in range(1, 4):
                @pl.when(jnp.logical_and(n == 2 * s - 1, same))
                def _(s=s):
                    lstep(s, 1)

            @pl.when(n == jnp.where(same, 7, 1))
            def _():
                lstep(4)

            @pl.when(jnp.logical_and(n % 2 == 1, same))
            def _():
                meta_in(n)

                @pl.when(n < NY - 1)
                def _():
                    meta_in(n + 1)

            meta_copy(n).wait()

            @pl.when(jnp.logical_and(n % 2 == 0, differs))
            def _():
                meta_in(n + 1)

                @pl.when(n < NY - 2)
                def _():
                    meta_in(n + 2)

            compute(n)
            zcopy(n).start()

        @pl.when(jnp.logical_and(n >= LAG, n < NY + LAG))
        def _():
            finish(n - LAG)

        @pl.when(n >= 2 * LAG)
        def _():
            combine(n - 2 * LAG)
        return carry

    lax.fori_loop(0, NY + 2 * LAG, main, 0)

    for c in sent:
        describe(*c).wait_send()
    for h in range(2):
        for c in pair_copies(h):
            c.wait_send()
    for s in range(1, 5):
        for h, slot, copies in lring(s):
            for c in copies:
                c.wait_send()

    @pl.when(jnp.logical_not(keeps_own))
    def _():
        for c in near_copies():
            c.wait_send()

    @pl.when(is_base)
    def _():
        for k in range(4):
            for c in xcopies(k):
                c.wait_send()

    @pl.when(jnp.logical_not(is_base))
    def _():
        for k in range(4):
            sec, a, b = hops(k)
            a.wait_send()
            b.wait_send()

    def drain(n, carry):
        zcopy(n).wait_send()

        @pl.when(n > 0)
        def _():
            ycopy(n).wait_send()
        return carry

    lax.fori_loop(0, NY, drain, 0)


def local(p_vals, p_cols, f_cols):
    vals = p_vals.reshape(RB, 3, 2, BS, BS)
    left = vals.transpose(0, 1, 3, 2, 4).reshape(NT, BS, TW)
    right = vals.transpose(0, 1, 4, 2, 3).reshape(NT, BS, TW)
    keys = p_cols[:, 0]
    slot = jnp.arange(SLOT, dtype=jnp.int32)[None]
    place = jnp.arange(RB, dtype=jnp.int32)[:, None] * 3 + slot // 2
    hit = keys[:, None, :] == jnp.arange(32, dtype=jnp.int32)[None, :, None]
    lo = jnp.min(jnp.where(hit, (place + slot % 2 * NT)[:, None], 2 * NT), axis=2)
    hi = jnp.min(jnp.where(hit, (place + (1 - slot % 2) * NT)[:, None], 2 * NT), axis=2)
    row_data = jnp.concatenate([lo, hi, jnp.pad(keys, ((0, 0), (0, 64 - SLOT)))], axis=1)
    meta = jnp.concatenate([f_cols.reshape(RB, 128), row_data], axis=0)

    vm = pl.BlockSpec(memory_space=pltpu.VMEM)
    bf, f32 = jnp.bfloat16, jnp.float32
    out = pl.pallas_call(
        kernel,
        out_shape=jax.ShapeDtypeStruct((RB * NY, BS, TW), f32),
        in_specs=[vm] * 3,
        out_specs=vm,
        scratch_shapes=[
            pltpu.VMEM((4 * NY * NT, BS, TW), bf),
            pltpu.VMEM((8 * SEC, BS, TW), bf),
            pltpu.VMEM((SEC, BS, TW), bf),
            pltpu.VMEM((4 * NY, 8, 128), jnp.int32),
            pltpu.VMEM((8, 8, 128), jnp.int32),
            pltpu.SMEM((4 * NY, 8, 128), jnp.int32),
            pltpu.SMEM((8, 8, 128), jnp.int32),
            pltpu.SMEM((8, 128), jnp.int32),
            pltpu.VMEM((2, 4 * SLOT * BS, 2 * TW), bf),
            pltpu.VMEM((NY, RB * BS, TW), f32),
            pltpu.VMEM((NY, RB * BS, TW), bf),
            pltpu.VMEM((NY, RB * BS, TW), bf),
            pltpu.VMEM((NY, RB * BS, TW), bf),
            pltpu.VMEM((NY, RB * BS, TW), bf),
            pltpu.SemaphoreType.DMA((176,)),
            pltpu.SemaphoreType.DMA((4 * NY, 2)),
            pltpu.SemaphoreType.DMA((4 * NY,)),
            pltpu.SemaphoreType.DMA((8,)),
            pltpu.SemaphoreType.DMA((8,)),
            pltpu.SemaphoreType.DMA((NY,)),
            pltpu.SemaphoreType.DMA((NY,)),
            pltpu.SemaphoreType.DMA((NY,)),
            pltpu.SemaphoreType.DMA((NY,)),
            pltpu.SemaphoreType.DMA((4,)),
        ],
        compiler_params=pltpu.CompilerParams(
            collective_id=0, has_side_effects=True, vmem_limit_bytes=48 * 1024 * 1024),
    )(left, right, meta)
    out = out.reshape(RB, NY, BS // 2, 2, TW).transpose(0, 1, 3, 2, 4)
    return out.reshape(RB, 1, NY, 2, BS * BS)


def solution(mesh):
    return jax.shard_map(
        local,
        mesh=mesh,
        in_specs=(
            P(("row", "col"), "rep", None, None),
            P(("row", "col"), "rep", None),
            P(("row", "col"), None, None, None),
        ),
        out_specs=P(("row", "col"), "rep", None, None, None),
        check_vma=False,
    )
```
